32 devices in a mesh: case: 2 (over x), tile: 16 (over z, y, core).
Axes of the slice: x: 2, y: 2, z: 4, core: 2. Of those that a mesh axis runs over, the one named last changes fastest.
Arguments:
- node_coords: float32 [256, 3, 512], P(('case', 'tile')), parts along dimension 0, may hold values from 0 to 2.8
- node_sens: float32 [256, 3, 512], P(('case', 'tile')), parts along dimension 0, may hold values from -1.5 to 1.5
- centre_coords: float32 [3, 61440], P(None, ('case', 'tile')), parts along dimension 1, may hold values from 0 to 2.8
- centre_weights: float32 [3, 61440], P(None, ('case', 'tile')), parts along dimension 1, may hold values from -4 to 4
- pair_list: int32 [2, 8192], P(None, ('case', 'tile')), parts along dimension 1, may hold values from 0 to 239, as said below
- pair_count: int32 [32], P(('case', 'tile')), parts along dimension 0, may hold values from 1 to 256, as said below
Outputs:
- weight_grad: float32 [3, 61440], P(None, ('case', 'tile')), parts along dimension 1
- centre_grad: float32 [3, 61440], P(None, ('case', 'tile')), parts along dimension 1
The draws below stay inside these ranges and needn't reach their ends.
There are 2 independent parts, one for each index of `case`. The reference program is written for one: setup_inputs(seed, part) draws one part's arguments, and reference() takes and returns one part's arrays. A program takes and returns all parts, laid end to end along the dimension named above; each array names one. Nothing has to cross between parts.
Inputs may be any that keep to these rules, and one draw needn't show every extreme that they name: `pair_list`: row 0 holds centre blocks; a slot of device d names only blocks b with d - 2 <= b // 15 <= d + 2. Row 1 holds tiles 0 to 7. `pair_count`: at most 256 live slots a device, reached on some device; at least 1.
All inputs are finite; a program needn't handle non-finite values.
Results may differ from the reference program's by a relative error of at most 0.0003.
Values sent between devices are 32-bit elements; how exact they have to be, the bound alone decides.
No kernel may reach another device: no remote copies, remote signals or barrier semaphores. Data moves between devices by JAX's collectives and lax.ppermute only.
A program may use at most 64 MiB of HBM per device.

```python
import jax
import jax.numpy as jnp
from jax import lax

TILE_NODES = 512
CENTRE_BLOCK = 128
CB_DEV = 15
TILES_DEV = 8
PAIRS_DEV = 256
NB = 240
NC = 30720
NTILES = 128
NPAIRS = 4096
N_TILE = 16


def draw_pair_count(key, part):
    key = jax.random.fold_in(key, 11)
    device = jnp.arange(N_TILE, dtype=jnp.int32)
    upper = PAIRS_DEV // (1 + 3 * device // N_TILE)
    lower = jnp.maximum(upper // 2, 1)
    count = jax.random.randint(key, (N_TILE,), lower, upper + 1)
    return count.at[0].set(PAIRS_DEV).astype(jnp.int32)


def draw_pair_list(key, part):
    key = jax.random.fold_in(key, 12)
    first, second = jax.random.split(key)
    slots = jnp.arange(N_TILE * PAIRS_DEV, dtype=jnp.int32)
    device = slots // PAIRS_DEV
    nearby = jax.random.randint(first, slots.shape, -2 * CB_DEV, 3 * CB_DEV)
    blocks = jnp.clip(device * CB_DEV + nearby, 0, CB_DEV * N_TILE - 1)
    tiles = jax.random.randint(second, slots.shape, 0, TILES_DEV)
    return jnp.stack([blocks, tiles]).astype(jnp.int32)


def block_scale(rng, shape, shards, smallest, top_value):
    def one(dim, parts):
        steps = jax.random.uniform(jax.random.fold_in(jax.random.fold_in(rng, 6), dim), (parts,), jnp.float32, smallest / len(shards), top_value / len(shards))
        return jnp.repeat(jnp.exp(steps), shape[dim] // parts).reshape((-1,) + (1,) * (len(shape) - dim - 1))

    loudness = one(*shards[0])
    for cut in shards[1:]:
        loudness = loudness * one(*cut)
    return loudness


def normal_values(stream_key, shape, width, most, shards=(), kind=jnp.bfloat16):
    factor_of = block_scale(stream_key, shape, shards, -0.22, 0.18) if shards else 1.0
    drawn = jax.random.normal(stream_key, shape, jnp.float32) * width * factor_of
    return jnp.minimum(jnp.maximum(drawn, -most), most).astype(kind)


def setup_inputs(seed: int = 0, part: int = 0) -> dict:
    arg_keys = jax.random.split(jax.random.key(seed), 7)
    part_splits = jax.random.split(jax.random.fold_in(arg_keys[6], part), 7)
    return {
        "node_coords": jnp.clip(2.8 * jax.random.uniform(part_splits[0], (NTILES, 3, TILE_NODES), jnp.float32) ** block_scale(part_splits[0], (NTILES, 3, TILE_NODES), ((0, 16),), -0.2, 0.2), 0.0, 2.8),
        "node_sens": normal_values(part_splits[1], (NTILES, 3, TILE_NODES), 0.1, 1.5, ((0, 16),), jnp.float32),
        "centre_coords": jnp.clip(2.8 * jax.random.uniform(part_splits[2], (3, NC), jnp.float32) ** block_scale(part_splits[2], (3, NC), ((1, 16),), -0.2, 0.2), 0.0, 2.8),
        "centre_weights": normal_values(part_splits[3], (3, NC), 0.3, 4.0, ((1, 16),), jnp.float32),
        "pair_list": draw_pair_list(jax.random.fold_in(jax.random.fold_in(arg_keys[6], part), 71), part),
        "pair_count": draw_pair_count(jax.random.fold_in(jax.random.fold_in(arg_keys[6], part), 71), part),
    }


support = 2.0

def pair_terms(centres, nodes, sens):
    apart = centres[:3, :, None] - nodes[:, None, :]
    radius = jnp.sqrt(lax.optimization_barrier(jnp.sum(apart * apart, axis=0))) / support
    remain = 1.0 - jnp.minimum(radius, 1.0)
    kernel = remain ** 4 * (4.0 * radius + 1.0)
    slope = -20.0 * remain ** 3 / (support * support)
    high = lax.Precision.HIGHEST
    weight_part = jnp.einsum('kv,cv->kc', sens, kernel, precision=high)
    coupled = jnp.einsum('kc,kv->cv', centres[3:], sens, precision=high)
    weighted = coupled * slope
    row_total = lax.optimization_barrier(jnp.sum(weighted, axis=1))
    moment = jnp.einsum('cv,kv->kc', weighted, nodes, precision=high)
    shape_part = centres[:3] * row_total[None, :] - moment
    return jnp.concatenate([weight_part, shape_part], axis=0)

def reference(node_coords, node_sens, centre_coords, centre_weights, pair_list, pair_count):
    table = jnp.concatenate([centre_coords, centre_weights], 0).reshape(6, NB, CENTRE_BLOCK)

    def step(totals, group):
        slots = group * 8 + jnp.arange(8, dtype=jnp.int32)
        device_of = slots // PAIRS_DEV
        live = slots % PAIRS_DEV < pair_count[device_of]
        blocks = pair_list[0, slots]
        tiles = device_of * TILES_DEV + pair_list[1, slots]
        centres = jnp.moveaxis(jnp.take(table, blocks, axis=1), 1, 0)
        terms = jax.vmap(pair_terms)(centres, node_coords[tiles], node_sens[tiles])
        terms = jnp.where(live[:, None, None], terms, jnp.float32(0.0))
        totals = totals.at[:, blocks].add(jnp.moveaxis(terms, 0, 1))
        return (totals, None)
    start = jnp.zeros((6, NB, CENTRE_BLOCK), jnp.float32)
    totals, _ = lax.scan(step, start, jnp.arange(NPAIRS // 8, dtype=jnp.int32))
    flat = totals.reshape(6, NB * CENTRE_BLOCK)
    return (flat[:3], flat[3:])
```

```python
import functools

import jax
import jax.numpy as jnp
from jax import lax
from jax.experimental import pallas as pl
from jax.experimental.pallas import tpu as pltpu
from jax.sharding import PartitionSpec as P

CENTRE_BLOCK = 128
REACH = 2
MIDDLE = 1.4
TINY = 1e-30

F32 = jnp.float32
BF16 = jnp.bfloat16


def from_behind(array, axis, by):
    devices = lax.axis_size(axis)
    pairs = [(i, i + by) for i in range(devices) if 0 <= i + by < devices]
    return lax.ppermute(array, axis, pairs)


def dot(a, b):
    return lax.dot_general(a, b, (((1,), (0,)), ((), ())), preferred_element_type=F32)


def split2(x):
    high = x.astype(BF16)
    return high, (x - high.astype(F32)).astype(BF16)


def split3(x):
    one = x.astype(BF16).astype(F32)
    rest = x - one
    two = rest.astype(BF16).astype(F32)
    return one, two, rest - two


def prepare_centres(centres, table_ref, block):
    a = (centres - MIDDLE) * 0.5
    norm = jnp.sum(a * a, axis=0, keepdims=True)
    a1, a2, a3 = split3(a * -2.0)
    n1, n2, n3 = split3(norm)
    ones = jnp.ones((3, CENTRE_BLOCK), F32)
    pad = jnp.zeros((5, CENTRE_BLOCK), F32)
    pad2 = jnp.zeros((2, CENTRE_BLOCK), F32)
    rows = [a1, pad, a2, pad, a3, pad, a1, pad, a2, pad, a1, pad, ones, n1, n2, n3, pad2, a3, pad]
    table_ref[block] = jnp.concatenate(rows, 0).astype(BF16)


def prepare_tile(packed, nodes_ref, sens_ref, tile):
    b = (packed - MIDDLE) * 0.5
    q1, q2, q3 = split3(b)
    place = b[0:3]
    n1, n2, n3 = split3(jnp.sum(place * place, axis=0, keepdims=True))
    width = packed.shape[1]
    norm = jnp.concatenate([n1, n2, n3, jnp.ones((3, width), F32), jnp.zeros((2, width), F32)], 0)
    rows = jnp.concatenate([q1, q1, q1, q2, q2, q3, norm, q2], 0).astype(BF16)
    nodes_ref[tile] = jnp.concatenate([rows, rows], 0).T
    sens = packed[3:6]
    moments = jnp.concatenate([sens] + [sens * place[j : j + 1] for j in range(3)], 0)
    sens_high, sens_low = split2(sens)
    high, low = split2(moments)
    zeros = lambda n: jnp.zeros((n, width), F32)
    sens_ref[tile] = jnp.concatenate(
        [sens_high.astype(F32), sens_low.astype(F32), zeros(10), high.astype(F32), low.astype(F32), zeros(8)], 0
    ).astype(BF16)


def list_pairs(codes, first, blocks, rows):
    slots = 8 * blocks
    lanes = CENTRE_BLOCK
    j_row = lax.broadcasted_iota(jnp.int32, (lanes, lanes), 0)
    j_col = lax.broadcasted_iota(jnp.int32, (lanes, lanes), 1)
    before = (j_col < j_row).astype(F32).astype(BF16)
    ones = jnp.ones((codes[0].shape[1], lanes), BF16)
    base = jnp.zeros((1, lanes), F32)
    listed = [jnp.zeros((1, lanes), F32)] * rows
    j_wide = lax.broadcasted_iota(jnp.int32, (lanes, codes[0].shape[1]), 0)
    for source, row in enumerate(codes):
        local = row.astype(jnp.int32) - 1 - 8 * first
        hit = ((local == j_wide) & (j_wide < slots)).astype(F32).astype(BF16)
        times = dot(hit, ones)
        active = times > 0.0
        flag = active.astype(F32)
        position = dot(before, flag.astype(BF16)) + base
        position = jnp.where(active, position, -1.0).astype(jnp.int32)
        value = (source * lanes + j_row).astype(F32) + 1024.0 * times
        for g in range(rows):
            here = jnp.where(position == j_col + g * lanes, value, 0.0)
            listed[g] = listed[g] + jnp.sum(here, axis=0, keepdims=True)
        base = base + jnp.sum(flag, axis=0, keepdims=True)
    fill = [jnp.zeros((1, lanes), F32)] * (7 - rows)
    return jnp.concatenate(listed + [base] + fill, 0).astype(jnp.int32)


def profile(s):
    s = jnp.minimum(jnp.maximum(s, TINY), 1.0)
    r = s * lax.rsqrt(s)
    u = 1.0 - r
    u2 = u * u
    u3 = u2 * u
    u4 = u2 * u2
    return u4 * (0.25 + r), u3


def run_pairs(list_ref, count, table_ref, nodes_ref, sens_ref, total_ref, s0, s1, f0, f1):
    def item(k):
        value = list_ref[k // 128, k % 128]
        code = value % 1024
        tile = (code // 128) * 8 + code % 8
        block = (code % 128) // 8
        return tile, block, (value // 1024).astype(F32)

    def items(p):
        p = jnp.maximum(p, 0)
        return item(2 * p), item(2 * p + 1)

    lane = lax.broadcasted_iota(jnp.int32, (512, 128), 1)

    def distances(p, out):
        (t1, b1, _), (t2, b2, _) = items(p)
        zero = jnp.zeros((64, 128), BF16)
        rhs = jnp.concatenate(
            [jnp.concatenate([table_ref[b1], zero], 1), jnp.concatenate([zero, table_ref[b2]], 1)], 0
        )
        lhs = jnp.where(lane < 64, nodes_ref[t1], nodes_ref[t2])
        out[...] = dot(lhs, rhs)

    def profiles(s_ref, out):
        for k in range(0, 512, 64):
            rows = slice(k, k + 64)
            kernel, slope = profile(s_ref[rows])
            out[0, rows], out[1, rows] = split2(kernel)
            out[2, rows], out[3, rows] = split2(slope)

    def sums(p, f_ref):
        (t1, b1, m1), (t2, b2, m2) = items(p)
        left, right = sens_ref[t1], sens_ref[t2]
        mk = jnp.concatenate([left[0:16], right[0:16]], 0)
        mu = jnp.concatenate([left[16:48], right[16:48]], 0)
        kernel = dot(mk, f_ref[0]) + dot(mk, f_ref[1])
        slope = dot(mu, f_ref[2]) + dot(mu, f_ref[3])
        total_ref[b1, 0:16] += m1 * kernel[0:16, :128]
        total_ref[b1, 16:48] += m1 * slope[0:32, :128]
        total_ref[b2, 0:16] += m2 * kernel[16:32, 128:]
        total_ref[b2, 16:48] += m2 * slope[32:64, 128:]

    steps = (count + 7) // 8

    @pl.when(steps > 0)
    def _():
        distances(0, s0)
        f1[...] = jnp.zeros_like(f1)

        def step(j, carry):
            for half in (0, 2):
                p = 4 * j + half
                sums(p - 1, f1)
                distances(p + 1, s1)
                profiles(s0, f0)
                sums(p, f0)
                distances(p + 2, s0)
                profiles(s1, f1)
            return carry

        lax.fori_loop(0, steps, step, 0)
        sums(4 * steps - 1, f1)


def own_kernel(packed_ref, centres_ref, first_ref, total_ref, table_ref, *scratch):
    nodes_ref, sens_ref, list_vmem, list_smem, sem, s0, s1, f0, f1 = scratch
    blocks = table_ref.shape[0]
    for block in range(blocks):
        prepare_centres(centres_ref[:, block * 128 : (block + 1) * 128], table_ref, block)
    list_vmem[...] = list_pairs([packed_ref[0, 6:7, 0:256]], first_ref[0], blocks, 2)
    copy = pltpu.make_async_copy(list_vmem, list_smem, sem)
    copy.start()
    total_ref[...] = jnp.zeros_like(total_ref)
    for tile in range(8):
        prepare_tile(packed_ref[tile], nodes_ref, sens_ref, tile)
    copy.wait()
    run_pairs(list_smem, list_smem[2, 0], table_ref, nodes_ref, sens_ref, total_ref, s0, s1, f0, f1)


def near_kernel(p0, p1, p2, p3, centres_ref, weights_ref, first_ref, before_ref, table_ref, *rest):
    grad_w, grad_c, total_ref, nodes_ref, sens_ref, list_vmem, list_smem, sem, s0, s1, f0, f1 = rest
    packed = (p0, p1, p2, p3)
    blocks = table_ref.shape[0]
    list_vmem[...] = list_pairs([p[0, 6:7, 0:256] for p in packed], first_ref[0], blocks, 5)
    copy = pltpu.make_async_copy(list_vmem, list_smem, sem)
    copy.start()
    total_ref[...] = before_ref[...]
    for source, ref in enumerate(packed):
        for tile in range(8):
            prepare_tile(ref[tile], nodes_ref, sens_ref, source * 8 + tile)
    copy.wait()
    run_pairs(list_smem, list_smem[5, 0], table_ref, nodes_ref, sens_ref, total_ref, s0, s1, f0, f1)
    for block in range(blocks):
        total = total_ref[block]
        here = slice(block * 128, (block + 1) * 128)
        grad_w[:, here] = 4.0 * (total[0:3] + total[3:6])
        both = total[16:28] + total[28:40]
        a = (centres_ref[:, here] - MIDDLE) * 0.5
        w = weights_ref[:, here] * -10.0
        for j in range(3):
            terms = w * (a[j : j + 1] * both[0:3] - both[3 + 3 * j : 6 + 3 * j])
            grad_c[j : j + 1, here] = jnp.sum(terms, axis=0, keepdims=True)


def body(node_coords, node_sens, centre_coords, centre_weights, pair_list, pair_count):
    device = lax.axis_index("tile")
    tiles, _, nodes = node_coords.shape
    slots = pair_list.shape[1]
    blocks = centre_coords.shape[1] // CENTRE_BLOCK
    code = pair_list[0] * 8 + pair_list[1] + 1
    code = jnp.where(jnp.arange(slots) < pair_count[0], code, 0).astype(F32)
    last = jnp.zeros((tiles, 2, nodes), F32).at[0, 0, :slots].set(code)
    packed = jnp.concatenate([node_coords, node_sens, last], 1)
    near = [from_behind(packed, "tile", by) for by in (1, -1, 2, -2)]
    first = (device * blocks).astype(jnp.int32).reshape(1)

    vmem = pl.BlockSpec(memory_space=pltpu.VMEM)
    smem = pl.BlockSpec(memory_space=pltpu.SMEM)

    def scratch(count):
        return [
            pltpu.VMEM((count, nodes, 128), BF16),
            pltpu.VMEM((count, 48, nodes), BF16),
            pltpu.VMEM((8, 128), jnp.int32),
            pltpu.SMEM((8, 128), jnp.int32),
            pltpu.SemaphoreType.DMA,
            pltpu.VMEM((nodes, 256), F32),
            pltpu.VMEM((nodes, 256), F32),
            pltpu.VMEM((4, nodes, 256), BF16),
            pltpu.VMEM((4, nodes, 256), BF16),
        ]

    params = pltpu.CompilerParams(vmem_limit_bytes=40 << 20)
    total_type = jax.ShapeDtypeStruct((blocks, 48, 128), F32)
    own, table = pl.pallas_call(
        own_kernel,
        out_shape=(total_type, jax.ShapeDtypeStruct((blocks, 64, 128), BF16)),
        in_specs=[vmem, vmem, smem],
        out_specs=(vmem, vmem),
        scratch_shapes=scratch(tiles),
        compiler_params=params,
        cost_estimate=pl.CostEstimate(flops=10**9, bytes_accessed=10**6, transcendentals=0),
        name="own_pairs",
    )(packed, centre_coords, first)
    grads = jax.ShapeDtypeStruct(centre_coords.shape, F32)
    return pl.pallas_call(
        near_kernel,
        out_shape=(grads, grads),
        in_specs=[vmem] * 6 + [smem] + [vmem] * 2,
        out_specs=(vmem, vmem),
        scratch_shapes=[pltpu.VMEM((blocks, 48, 128), F32)] + scratch(4 * tiles),
        compiler_params=params,
        name="near_pairs",
    )(*near, centre_coords, centre_weights, first, own, table)


def solution(mesh):
    return jax.shard_map(
        body,
        mesh=mesh,
        in_specs=(
            P(("case", "tile"), None, None),
            P(("case", "tile"), None, None),
            P(None, ("case", "tile")),
            P(None, ("case", "tile")),
            P(None, ("case", "tile")),
            P(("case", "tile")),
        ),
        out_specs=(P(None, ("case", "tile")), P(None, ("case", "tile"))),
        check_vma=False,
    )
```

```python
import functools

import jax
import jax.numpy as jnp
from jax import lax
from jax.experimental import pallas as pl
from jax.experimental.pallas import tpu as pltpu
from jax.sharding import PartitionSpec as P

CENTRE_BLOCK = 128
REACH = 2
MIDDLE = 1.4
TINY = 1e-30

F32 = jnp.float32
BF16 = jnp.bfloat16


def swap(array, axis, by, phase):
    devices = lax.axis_size(axis)
    pairs = []
    for i in range(devices - by):
        if (i // by) % 2 == phase:
            pairs += [(i, i + by), (i + by, i)]
    return lax.ppermute(array, axis, pairs)


def dot(a, b):
    return lax.dot_general(a, b, (((1,), (0,)), ((), ())), preferred_element_type=F32)


def split2(x):
    high = x.astype(BF16)
    return high, (x - high.astype(F32)).astype(BF16)


def split3(x):
    one = x.astype(BF16).astype(F32)
    rest = x - one
    two = rest.astype(BF16).astype(F32)
    return one, two, rest - two


def prepare_centres(centres, table_ref, block):
    a = (centres - MIDDLE) * 0.5
    norm = jnp.sum(a * a, axis=0, keepdims=True)
    a1, a2, a3 = split3(a * -2.0)
    n1, n2, n3 = split3(norm)
    ones = jnp.ones((3, CENTRE_BLOCK), F32)
    pad = jnp.zeros((2, CENTRE_BLOCK), F32)
    rows = [a1, a2, a3, a1, a2, a1, ones, n1, n2, n3, a3, a2, pad]
    table_ref[block] = jnp.concatenate(rows, 0).astype(BF16)


def prepare_source(packed_ref, nodes_ref, sens_ref, rows_ref, source):
    place = [(packed_ref[j] - MIDDLE) * 0.5 for j in range(3)]
    sens = [packed_ref[3 + k] for k in range(3)]
    parts = [split3(x) for x in place]
    q1, q2, q3 = ([p[i] for p in parts] for i in range(3))
    norm = split3(place[0] * place[0] + place[1] * place[1] + place[2] * place[2])
    one = jnp.ones_like(place[0])
    zero = jnp.zeros_like(one)
    groups = one.shape[1] // 128
    kinds = q1 * 3 + q2 * 2 + q3 + list(norm) + [one] * 3 + q2 + q3 + [zero] * 2
    moments = sens + [s * place[j] for j in range(3) for s in sens]
    halves = [split2(m) for m in moments]
    high = [h.astype(F32) for h, _ in halves]
    low = [l.astype(F32) for _, l in halves]
    kinds += high[:3] + low[:3] + [zero] * 10 + high + low + [zero] * 8
    for kind, value in enumerate(kinds):
        for g in range(groups):
            rows_ref[g, 8 * kind : 8 * kind + 8] = value[:, g * 128 : (g + 1) * 128]
    for t in range(8):
        for g in range(groups):
            lanes = slice(g * 128, (g + 1) * 128)
            rows = rows_ref[g, pl.ds(t, 32, stride=8), :].astype(BF16)
            nodes_ref[8 * source + t, lanes] = jnp.concatenate([rows, rows], 0).T
            sens_ref[8 * source + t, :, lanes] = rows_ref[g, pl.ds(256 + t, 48, stride=8), :].astype(BF16)


def list_pairs(codes, first, blocks, rows):
    slots = 8 * blocks
    lanes = CENTRE_BLOCK
    j_row = lax.broadcasted_iota(jnp.int32, (lanes, lanes), 0)
    j_col = lax.broadcasted_iota(jnp.int32, (lanes, lanes), 1)
    before = (j_col < j_row).astype(F32).astype(BF16)
    ones = jnp.ones((codes[0].shape[1], lanes), BF16)
    base = jnp.zeros((1, lanes), F32)
    listed = [jnp.zeros((1, lanes), F32)] * rows
    j_wide = lax.broadcasted_iota(jnp.int32, (lanes, codes[0].shape[1]), 0)
    for source, row in enumerate(codes):
        local = row.astype(jnp.int32) - 1 - 8 * first
        hit = ((local == j_wide) & (j_wide < slots)).astype(F32).astype(BF16)
        times = dot(hit, ones)
        active = times > 0.0
        flag = active.astype(F32)
        position = dot(before, flag.astype(BF16)) + base
        position = jnp.where(active, position, -1.0).astype(jnp.int32)
        value = (source * lanes + j_row).astype(F32) + 1024.0 * times
        for g in range(rows):
            here = jnp.where(position == j_col + g * lanes, value, 0.0)
            listed[g] = listed[g] + jnp.sum(here, axis=0, keepdims=True)
        base = base + jnp.sum(flag, axis=0, keepdims=True)
    fill = [jnp.zeros((1, lanes), F32)] * (7 - rows)
    return jnp.concatenate(listed + [base] + fill, 0).astype(jnp.int32)


def profile(s):
    s = jnp.minimum(jnp.maximum(s, TINY), 1.0)
    r = s * lax.rsqrt(s)
    u = 1.0 - r
    u2 = u * u
    u3 = u2 * u
    u4 = u2 * u2
    return u4 * (0.25 + r), u3


def run_pairs(list_ref, count, table_ref, nodes_ref, sens_ref, total_ref, s0, s1, f0, f1):
    def item(k):
        value = list_ref[k // 128, k % 128]
        code = value % 1024
        tile = (code // 128) * 8 + code % 8
        block = (code % 128) // 8
        return tile, block, (value // 1024).astype(F32)

    def items(p):
        p = jnp.maximum(p, 0)
        return item(2 * p), item(2 * p + 1)

    lane = lax.broadcasted_iota(jnp.int32, (512, 64), 1)

    def distances(p, out):
        (t1, b1, _), (t2, b2, _) = items(p)
        zero = jnp.zeros((32, 128), BF16)
        rhs = jnp.concatenate(
            [jnp.concatenate([table_ref[b1], zero], 1), jnp.concatenate([zero, table_ref[b2]], 1)], 0
        )
        lhs = jnp.where(lane < 32, nodes_ref[t1], nodes_ref[t2])
        out[...] = dot(lhs, rhs)

    def profiles(s_ref, out):
        for k in range(0, 512, 64):
            rows = slice(k, k + 64)
            kernel, slope = profile(s_ref[rows])
            out[0, rows], out[1, rows] = split2(kernel)
            out[2, rows], out[3, rows] = split2(slope)

    def sums(p, f_ref):
        (t1, b1, m1), (t2, b2, m2) = items(p)
        left, right = sens_ref[t1], sens_ref[t2]
        mk = jnp.concatenate([left[0:16], right[0:16]], 0)
        mu = jnp.concatenate([left[16:48], right[16:48]], 0)
        kernel = dot(mk, f_ref[0]) + dot(mk, f_ref[1])
        slope = dot(mu, f_ref[2]) + dot(mu, f_ref[3])
        total_ref[b1, 0:16] += m1 * kernel[0:16, :128]
        total_ref[b1, 16:48] += m1 * slope[0:32, :128]
        total_ref[b2, 0:16] += m2 * kernel[16:32, 128:]
        total_ref[b2, 16:48] += m2 * slope[32:64, 128:]

    steps = (count + 7) // 8

    @pl.when(steps > 0)
    def _():
        distances(0, s0)
        f1[...] = jnp.zeros_like(f1)

        def step(j, carry):
            for half in (0, 2):
                p = 4 * j + half
                sums(p - 1, f1)
                distances(p + 1, s1)
                profiles(s0, f0)
                sums(p, f0)
                distances(p + 2, s0)
                profiles(s1, f1)
            return carry

        lax.fori_loop(0, steps, step, 0)
        sums(4 * steps - 1, f1)


def own_kernel(packed_ref, centres_ref, first_ref, total_ref, table_ref, *scratch):
    nodes_ref, sens_ref, rows_ref, list_vmem, list_smem, sem, s0, s1, f0, f1 = scratch
    blocks = table_ref.shape[0]
    for block in range(blocks):
        prepare_centres(centres_ref[:, block * 128 : (block + 1) * 128], table_ref, block)
    list_vmem[...] = list_pairs([packed_ref[6, 0:1, 0:256]], first_ref[0], blocks, 2)
    copy = pltpu.make_async_copy(list_vmem, list_smem, sem)
    copy.start()
    total_ref[...] = jnp.zeros_like(total_ref)
    prepare_source(packed_ref, nodes_ref, sens_ref, rows_ref.at[0], 0)
    copy.wait()
    run_pairs(list_smem, list_smem[2, 0], table_ref, nodes_ref, sens_ref, total_ref, s0, s1, f0, f1)


def near_kernel(p0, p1, p2, p3, centres_ref, weights_ref, first_ref, before_ref, table_ref, *rest):
    grad_w, grad_c, total_ref, nodes_ref, sens_ref, rows_ref, list_vmem, list_smem, sem, s0, s1, f0, f1 = rest
    packed = (p0, p1, p2, p3)
    blocks = table_ref.shape[0]
    list_vmem[...] = list_pairs([p[6, 0:1, 0:256] for p in packed], first_ref[0], blocks, 5)
    copy = pltpu.make_async_copy(list_vmem, list_smem, sem)
    copy.start()
    total_ref[...] = before_ref[...]
    for source, ref in enumerate(packed):
        prepare_source(ref, nodes_ref, sens_ref, rows_ref.at[source], source)
    copy.wait()
    run_pairs(list_smem, list_smem[5, 0], table_ref, nodes_ref, sens_ref, total_ref, s0, s1, f0, f1)
    for block in range(blocks):
        total = total_ref[block]
        here = slice(block * 128, (block + 1) * 128)
        grad_w[:, here] = 4.0 * (total[0:3] + total[3:6])
        both = total[16:28] + total[28:40]
        a = (centres_ref[:, here] - MIDDLE) * 0.5
        w = weights_ref[:, here] * -10.0
        for j in range(3):
            terms = w * (a[j : j + 1] * both[0:3] - both[3 + 3 * j : 6 + 3 * j])
            grad_c[j : j + 1, here] = jnp.sum(terms, axis=0, keepdims=True)


def body(node_coords, node_sens, centre_coords, centre_weights, pair_list, pair_count):
    device = lax.axis_index("tile")
    tiles, _, nodes = node_coords.shape
    slots = pair_list.shape[1]
    blocks = centre_coords.shape[1] // CENTRE_BLOCK
    code = pair_list[0] * 8 + pair_list[1] + 1
    code = jnp.where(jnp.arange(slots) < pair_count[0], code, 0).astype(F32)
    code = jnp.pad(code[None, None], ((0, 0), (0, tiles - 1), (0, nodes - slots)))
    packed = jnp.concatenate([node_coords.transpose(1, 0, 2), node_sens.transpose(1, 0, 2), code], 0)
    near = [swap(packed, "tile", by, phase) for by in (1, 2) for phase in (0, 1)]
    first = (device * blocks).astype(jnp.int32).reshape(1)

    vmem = pl.BlockSpec(memory_space=pltpu.VMEM)
    smem = pl.BlockSpec(memory_space=pltpu.SMEM)

    def scratch(count):
        return [
            pltpu.VMEM((count, nodes, 64), BF16),
            pltpu.VMEM((count, 48, nodes), BF16),
            pltpu.VMEM((count // 8, nodes // 128, 80 * 8, 128), F32),
            pltpu.VMEM((8, 128), jnp.int32),
            pltpu.SMEM((8, 128), jnp.int32),
            pltpu.SemaphoreType.DMA,
            pltpu.VMEM((nodes, 256), F32),
            pltpu.VMEM((nodes, 256), F32),
            pltpu.VMEM((4, nodes, 256), BF16),
            pltpu.VMEM((4, nodes, 256), BF16),
        ]

    params = pltpu.CompilerParams(vmem_limit_bytes=40 << 20)
    total_type = jax.ShapeDtypeStruct((blocks, 48, 128), F32)
    own, table = pl.pallas_call(
        own_kernel,
        out_shape=(total_type, jax.ShapeDtypeStruct((blocks, 32, 128), BF16)),
        in_specs=[vmem, vmem, smem],
        out_specs=(vmem, vmem),
        scratch_shapes=scratch(tiles),
        compiler_params=params,
        cost_estimate=pl.CostEstimate(flops=10**9, bytes_accessed=10**6, transcendentals=0),
        name="own_pairs",
    )(packed, centre_coords, first)
    grads = jax.ShapeDtypeStruct(centre_coords.shape, F32)
    return pl.pallas_call(
        near_kernel,
        out_shape=(grads, grads),
        in_specs=[vmem] * 6 + [smem] + [vmem] * 2,
        out_specs=(vmem, vmem),
        scratch_shapes=[pltpu.VMEM((blocks, 48, 128), F32)] + scratch(4 * tiles),
        compiler_params=params,
        name="near_pairs",
    )(*near, centre_coords, centre_weights, first, own, table)


def solution(mesh):
    return jax.shard_map(
        body,
        mesh=mesh,
        in_specs=(
            P(("case", "tile"), None, None),
            P(("case", "tile"), None, None),
            P(None, ("case", "tile")),
            P(None, ("case", "tile")),
            P(None, ("case", "tile")),
            P(("case", "tile")),
        ),
        out_specs=(P(None, ("case", "tile")), P(None, ("case", "tile"))),
        check_vma=False,
    )
```

```python
import functools

import jax
import jax.numpy as jnp
from jax import lax
from jax.experimental import pallas as pl
from jax.experimental.pallas import tpu as pltpu
from jax.sharding import PartitionSpec as P

CENTRE_BLOCK = 128
REACH = 2
MIDDLE = 1.4
SCALE = 8.0
TINY = 1e-30

F32 = jnp.float32
BF16 = jnp.bfloat16
F8 = jnp.float8_e4m3fn


def swap(array, axis, by, phase):
    devices = lax.axis_size(axis)
    pairs = []
    for i in range(devices - by):
        if (i // by) % 2 == phase:
            pairs += [(i, i + by), (i + by, i)]
    return lax.ppermute(array, axis, pairs)


def dot(a, b):
    return lax.dot_general(a, b, (((1,), (0,)), ((), ())), preferred_element_type=F32)


def split2(x):
    high = x.astype(BF16)
    return high, (x - high.astype(F32)).astype(BF16)


def split3(x):
    one = x.astype(BF16).astype(F32)
    rest = x - one
    two = rest.astype(BF16).astype(F32)
    return one, two, rest - two


def prepare_centres(centres, table_ref, block):
    a = (centres - MIDDLE) * (SCALE / 2)
    norm = jnp.sum(a * a, axis=0, keepdims=True)
    a1, a2, a3 = split3(a * -2.0)
    n1, n2, n3 = split3(norm)
    ones = jnp.ones((3, CENTRE_BLOCK), F32)
    pad = jnp.zeros((2, CENTRE_BLOCK), F32)
    rows = [a1, a2, a3, a1, a2, a1, ones, n1, n2, n3, a3, a2, pad]
    table_ref[block] = jnp.concatenate(rows, 0).astype(BF16)


def prepare_source(packed_ref, nodes_ref, sens_ref, small_ref, inverse_ref, rows_ref, source):
    place = [(packed_ref[j] - MIDDLE) * (SCALE / 2) for j in range(3)]
    sens = [packed_ref[3 + k] for k in range(3)]
    parts = [split3(x) for x in place]
    q1, q2, q3 = ([p[i] for p in parts] for i in range(3))
    norm = split3(place[0] * place[0] + place[1] * place[1] + place[2] * place[2])
    one = jnp.ones_like(place[0])
    zero = jnp.zeros_like(one)
    groups = one.shape[1] // 128
    kinds = q1 * 3 + q2 * 2 + q3 + list(norm) + [one] * 3 + q2 + q3 + [zero] * 2
    moments = sens + [s * place[j] for j in range(3) for s in sens]
    halves = [split2(m) for m in moments]
    high = [h.astype(F32) for h, _ in halves]
    low = [l.astype(F32) for _, l in halves]
    kinds += high[:3] + low[:3] + [zero] * 10 + high + low + [zero] * 8
    largest = functools.reduce(jnp.maximum, [jnp.abs(m) for m in moments])
    largest = jnp.maximum(jnp.max(largest, axis=(0, 1), keepdims=True), TINY)
    inverse_ref[source] = jnp.broadcast_to(largest * (1.0 / 128.0), (8, 128))
    small = [m * (128.0 / largest) for m in moments]
    upper = [m.astype(F8).astype(F32) for m in small]
    kinds += upper + [m - h for m, h in zip(small, upper)] + [zero] * 8
    for kind, value in enumerate(kinds):
        for g in range(groups):
            rows_ref[g, 8 * kind : 8 * kind + 8] = value[:, g * 128 : (g + 1) * 128]
    for t in range(8):
        for g in range(groups):
            lanes = slice(g * 128, (g + 1) * 128)
            rows = rows_ref[g, pl.ds(t, 32, stride=8), :].astype(BF16)
            nodes_ref[8 * source + t, lanes] = jnp.concatenate([rows, rows], 0).T
            sens_ref[8 * source + t, :, lanes] = rows_ref[g, pl.ds(256 + t, 48, stride=8), :].astype(BF16)
            small_ref[8 * source + t, :, lanes] = rows_ref[g, pl.ds(640 + t, 32, stride=8), :].astype(F8)


def list_pairs(codes, first, blocks, rows):
    slots = 8 * blocks
    lanes = CENTRE_BLOCK
    j_row = lax.broadcasted_iota(jnp.int32, (lanes, lanes), 0)
    j_col = lax.broadcasted_iota(jnp.int32, (lanes, lanes), 1)
    before = (j_col < j_row).astype(F32).astype(BF16)
    ones = jnp.ones((codes[0].shape[1], lanes), BF16)
    base = jnp.zeros((1, lanes), F32)
    listed = [jnp.zeros((1, lanes), F32)] * rows
    j_wide = lax.broadcasted_iota(jnp.int32, (lanes, codes[0].shape[1]), 0)
    for source, row in enumerate(codes):
        local = row.astype(jnp.int32) - 1 - 8 * first
        hit = ((local == j_wide) & (j_wide < slots)).astype(F32).astype(BF16)
        times = dot(hit, ones)
        active = times > 0.0
        flag = active.astype(F32)
        position = dot(before, flag.astype(BF16)) + base
        position = jnp.where(active, position, -1.0).astype(jnp.int32)
        value = (source * lanes + j_row).astype(F32) + 1024.0 * times
        for g in range(rows):
            here = jnp.where(position == j_col + g * lanes, value, 0.0)
            listed[g] = listed[g] + jnp.sum(here, axis=0, keepdims=True)
        base = base + jnp.sum(flag, axis=0, keepdims=True)
    fill = [jnp.zeros((1, lanes), F32)] * (7 - rows)
    return jnp.concatenate(listed + [base] + fill, 0).astype(jnp.int32)


def profile(s):
    s = jnp.minimum(jnp.maximum(s, TINY), SCALE * SCALE)
    r = s * lax.rsqrt(s)
    u = SCALE - r
    u2 = u * u
    u3 = u2 * u
    u4 = u2 * u2
    return u4 * (SCALE / 4 + r), u3


def split_small(x):
    high = x.astype(BF16)
    return high, (x - high.astype(F32)).astype(F8)


def run_pairs(list_ref, count, table_ref, tables, total_ref, work):
    nodes_ref, sens_ref, small_ref, inverse_ref = tables
    s0, s1, f0, f1, g0, g1 = work

    def item(k):
        value = list_ref[k // 128, k % 128]
        code = value % 1024
        tile = (code // 128) * 8 + code % 8
        block = (code % 128) // 8
        return tile, block, (value // 1024).astype(F32), code // 128

    def items(p):
        p = jnp.maximum(p, 0)
        return item(2 * p), item(2 * p + 1)

    lane = lax.broadcasted_iota(jnp.int32, (512, 64), 1)

    def distances(p, out):
        (t1, b1, _, _), (t2, b2, _, _) = items(p)
        zero = jnp.zeros((32, 128), BF16)
        rhs = jnp.concatenate(
            [jnp.concatenate([table_ref[b1], zero], 1), jnp.concatenate([zero, table_ref[b2]], 1)], 0
        )
        lhs = jnp.where(lane < 32, nodes_ref[t1], nodes_ref[t2])
        out[...] = dot(lhs, rhs)

    def profiles(s_ref, out, low):
        for k in range(0, 512, 64):
            rows = slice(k, k + 64)
            kernel, slope = profile(s_ref[rows])
            out[0, rows], low[0, rows] = split_small(kernel)
            out[1, rows], low[1, rows] = split_small(slope)

    def sums(p, f_ref, g_ref):
        (t1, b1, m1, o1), (t2, b2, m2, o2) = items(p)
        left, right = sens_ref[t1], sens_ref[t2]
        kernel = dot(jnp.concatenate([left[0:16], right[0:16]], 0), f_ref[0])
        small = jnp.concatenate([small_ref[t1], small_ref[t2]], 0)
        kernel_low = dot(small, g_ref[0])
        slope = dot(jnp.concatenate([left[16:48], right[16:48]], 0), f_ref[1])
        slope_low = dot(small, g_ref[1])
        w1 = (m1 * inverse_ref[o1])[0:1]
        w2 = (m2 * inverse_ref[o2])[0:1]
        total_ref[b1, 0:8] += m1 * kernel[0:8, :128]
        total_ref[b1, 8:32] += m1 * slope[0:24, :128]
        total_ref[b1, 32:48] += w1 * kernel_low[0:16, :128]
        total_ref[b1, 48:72] += w1 * slope_low[0:24, :128]
        total_ref[b2, 0:8] += m2 * kernel[16:24, 128:]
        total_ref[b2, 8:32] += m2 * slope[32:56, 128:]
        total_ref[b2, 32:48] += w2 * kernel_low[32:48, 128:]
        total_ref[b2, 48:72] += w2 * slope_low[32:56, 128:]

    units = (count + 3) // 4

    @pl.when(units > 0)
    def _():
        distances(0, s0)
        f1[...] = jnp.zeros_like(f1)
        g1[...] = jnp.zeros_like(g1)

        def unit(j):
            p = 2 * j
            sums(p - 1, f1, g1)
            distances(p + 1, s1)
            profiles(s0, f0, g0)
            sums(p, f0, g0)
            distances(p + 2, s0)
            profiles(s1, f1, g1)

        def long_step(j, carry):
            for k in range(4):
                unit(4 * j + k)
            return carry

        def short_step(j, carry):
            unit(j)
            return carry

        lax.fori_loop(0, units // 4, long_step, 0)
        lax.fori_loop(units // 4 * 4, units, short_step, 0)
        sums(2 * units - 1, f1, g1)


def own_kernel(packed_ref, centres_ref, first_ref, total_ref, table_ref, *scratch):
    *tables, rows_ref, list_vmem, list_smem, sem = scratch[:8]
    work = scratch[8:]
    blocks = table_ref.shape[0]
    for block in range(blocks):
        prepare_centres(centres_ref[:, block * 128 : (block + 1) * 128], table_ref, block)
    list_vmem[...] = list_pairs([packed_ref[6, 0:1, 0:256]], first_ref[0], blocks, 2)
    copy = pltpu.make_async_copy(list_vmem, list_smem, sem)
    copy.start()
    total_ref[...] = jnp.zeros_like(total_ref)
    prepare_source(packed_ref, *tables, rows_ref.at[0], 0)
    copy.wait()
    run_pairs(list_smem, list_smem[2, 0], table_ref, tables, total_ref, work)


def near_kernel(p0, p1, p2, p3, centres_ref, weights_ref, first_ref, before_ref, table_ref, *rest):
    grad_w, grad_c, total_ref, *tables = rest[:7]
    rows_ref, list_vmem, list_smem, sem = rest[7:11]
    work = rest[11:]
    packed = (p0, p1, p2, p3)
    blocks = table_ref.shape[0]
    list_vmem[...] = list_pairs([p[6, 0:1, 0:256] for p in packed], first_ref[0], blocks, 5)
    copy = pltpu.make_async_copy(list_vmem, list_smem, sem)
    copy.start()
    total_ref[...] = before_ref[...]
    for source, ref in enumerate(packed):
        prepare_source(ref, *tables, rows_ref.at[source], source)
    copy.wait()
    run_pairs(list_smem, list_smem[5, 0], table_ref, tables, total_ref, work)
    for block in range(blocks):
        total = total_ref[block]
        here = slice(block * 128, (block + 1) * 128)
        grad_w[:, here] = (4.0 / SCALE**5) * (total[0:3] + total[3:6] + (total[32:35] + total[44:47]))
        both = total[8:20] + total[20:32] + (total[48:60] + total[60:72])
        a = (centres_ref[:, here] - MIDDLE) * (SCALE / 2)
        w = weights_ref[:, here] * (-10.0 / SCALE**4)
        for j in range(3):
            terms = w * (a[j : j + 1] * both[0:3] - both[3 + 3 * j : 6 + 3 * j])
            grad_c[j : j + 1, here] = jnp.sum(terms, axis=0, keepdims=True)


def body(node_coords, node_sens, centre_coords, centre_weights, pair_list, pair_count):
    device = lax.axis_index("tile")
    tiles, _, nodes = node_coords.shape
    slots = pair_list.shape[1]
    blocks = centre_coords.shape[1] // CENTRE_BLOCK
    code = pair_list[0] * 8 + pair_list[1] + 1
    code = jnp.where(jnp.arange(slots) < pair_count[0], code, 0).astype(F32)
    code = jnp.pad(code[None, None], ((0, 0), (0, tiles - 1), (0, nodes - slots)))
    packed = jnp.concatenate([node_coords.transpose(1, 0, 2), node_sens.transpose(1, 0, 2), code], 0)
    near = [swap(packed, "tile", by, phase) for by in (1, 2) for phase in (0, 1)]
    first = (device * blocks).astype(jnp.int32).reshape(1)

    vmem = pl.BlockSpec(memory_space=pltpu.VMEM)
    smem = pl.BlockSpec(memory_space=pltpu.SMEM)

    def scratch(count):
        return [
            pltpu.VMEM((count, nodes, 64), BF16),
            pltpu.VMEM((count, 48, nodes), BF16),
            pltpu.VMEM((count, 32, nodes), F8),
            pltpu.VMEM((count // 8, 8, 128), F32),
            pltpu.VMEM((count // 8, nodes // 128, 112 * 8, 128), F32),
            pltpu.VMEM((8, 128), jnp.int32),
            pltpu.SMEM((8, 128), jnp.int32),
            pltpu.SemaphoreType.DMA,
            pltpu.VMEM((nodes, 256), F32),
            pltpu.VMEM((nodes, 256), F32),
            pltpu.VMEM((2, nodes, 256), BF16),
            pltpu.VMEM((2, nodes, 256), BF16),
            pltpu.VMEM((2, nodes, 256), F8),
            pltpu.VMEM((2, nodes, 256), F8),
        ]

    params = pltpu.CompilerParams(vmem_limit_bytes=40 << 20)
    total_type = jax.ShapeDtypeStruct((blocks, 72, 128), F32)
    own, table = pl.pallas_call(
        own_kernel,
        out_shape=(total_type, jax.ShapeDtypeStruct((blocks, 32, 128), BF16)),
        in_specs=[vmem, vmem, smem],
        out_specs=(vmem, vmem),
        scratch_shapes=scratch(tiles),
        compiler_params=params,
        cost_estimate=pl.CostEstimate(flops=10**9, bytes_accessed=10**6, transcendentals=0),
        name="own_pairs",
    )(packed, centre_coords, first)
    grads = jax.ShapeDtypeStruct(centre_coords.shape, F32)
    return pl.pallas_call(
        near_kernel,
        out_shape=(grads, grads),
        in_specs=[vmem] * 6 + [smem] + [vmem] * 2,
        out_specs=(vmem, vmem),
        scratch_shapes=[pltpu.VMEM((blocks, 72, 128), F32)] + scratch(4 * tiles),
        compiler_params=params,
        name="near_pairs",
    )(*near, centre_coords, centre_weights, first, own, table)


def solution(mesh):
    return jax.shard_map(
        body,
        mesh=mesh,
        in_specs=(
            P(("case", "tile"), None, None),
            P(("case", "tile"), None, None),
            P(None, ("case", "tile")),
            P(None, ("case", "tile")),
            P(None, ("case", "tile")),
            P(("case", "tile")),
        ),
        out_specs=(P(None, ("case", "tile")), P(None, ("case", "tile"))),
        check_vma=False,
    )
```

```python
import functools

import jax
import jax.numpy as jnp
from jax import lax
from jax.experimental import pallas as pl
from jax.experimental.pallas import tpu as pltpu
from jax.sharding import PartitionSpec as P

CENTRE_BLOCK = 128
REACH = 2
MIDDLE = 1.4
SCALE = 8.0
TINY = 1e-30

F32 = jnp.float32
BF16 = jnp.bfloat16
F8 = jnp.float8_e4m3fn


def swap(array, axis, by, phase):
    devices = lax.axis_size(axis)
    pairs = []
    for i in range(devices - by):
        if (i // by) % 2 == phase:
            pairs += [(i, i + by), (i + by, i)]
    return lax.ppermute(array, axis, pairs)


def dot(a, b):
    return lax.dot_general(a, b, (((1,), (0,)), ((), ())), preferred_element_type=F32)


def split2(x):
    high = x.astype(BF16)
    return high, (x - high.astype(F32)).astype(BF16)


def split3(x):
    one = x.astype(BF16).astype(F32)
    rest = x - one
    two = rest.astype(BF16).astype(F32)
    return one, two, rest - two


def prepare_centres(centres, table_ref, block):
    a = (centres - MIDDLE) * (SCALE / 2)
    norm = jnp.sum(a * a, axis=0, keepdims=True)
    a1, a2, a3 = split3(a * -2.0)
    n1, n2, n3 = split3(norm)
    ones = jnp.ones((3, CENTRE_BLOCK), F32)
    zeros = jnp.zeros((2, CENTRE_BLOCK), F32)
    rows = [a1, a1, ones[:2], a2, a2, zeros, a3, a3, zeros, a1, ones[:1], n1, n2, n3, zeros[:1]]
    table_ref[block] = jnp.concatenate(rows, 0).astype(BF16)


def prepare_source(packed_ref, nodes_ref, sens_ref, small_ref, inverse_ref, rows_ref, source):
    place = [(packed_ref[j] - MIDDLE) * (SCALE / 2) for j in range(3)]
    sens = [packed_ref[3 + k] for k in range(3)]
    parts = [split3(x) for x in place]
    q1, q2, q3 = ([p[i] for p in parts] for i in range(3))
    norm = split3(place[0] * place[0] + place[1] * place[1] + place[2] * place[2])
    one = jnp.ones_like(place[0])
    zero = jnp.zeros_like(one)
    groups = one.shape[1] // 128
    empty = jnp.zeros((8, 128), F32)
    kinds = q1 + q2 + list(norm[:2]) + q3 + [norm[2], one, one, one, zero]
    moments = sens + [s * place[j] for j in range(3) for s in sens]
    halves = [split2(m) for m in moments]
    high = [h.astype(F32) for h, _ in halves]
    low = [l.astype(F32) for _, l in halves]
    kinds += high[:3] + low[:3] + high[3:] + low[3:]
    largest = functools.reduce(jnp.maximum, [jnp.abs(m) for m in moments])
    largest = jnp.maximum(jnp.max(largest, axis=(0, 1), keepdims=True), TINY)
    inverse_ref[source] = jnp.broadcast_to(largest * (1.0 / 128.0), (8, 128))
    small = [m * (128.0 / largest) for m in moments]
    upper = [m.astype(F8).astype(F32) for m in small]
    kinds += upper + [m - h for m, h in zip(small, upper)]
    for kind, value in enumerate(kinds):
        for g in range(groups):
            rows_ref[g, 8 * kind : 8 * kind + 8] = value[:, g * 128 : (g + 1) * 128]
    for t in range(8):
        for g in range(groups):
            lanes = slice(g * 128, (g + 1) * 128)
            rows = rows_ref[g, pl.ds(t, 16, stride=8), :]
            first, second = rows[0:8], rows[8:16]
            rows = jnp.concatenate([first, first, first, second], 0).astype(BF16)
            nodes_ref[8 * source + t, lanes] = jnp.concatenate([rows, rows], 0).T
            rows = jnp.concatenate([rows_ref[g, pl.ds(128 + t, 24, stride=8), :], empty], 0)
            sens_ref[8 * source + t, :, lanes] = rows.astype(BF16)
            rows = jnp.concatenate([rows_ref[g, pl.ds(320 + t, 24, stride=8), :], empty], 0)
            small_ref[8 * source + t, :, lanes] = rows.astype(F8)


def list_pairs(codes, first, blocks, rows):
    slots = 8 * blocks
    lanes = CENTRE_BLOCK
    j_row = lax.broadcasted_iota(jnp.int32, (lanes, lanes), 0)
    j_col = lax.broadcasted_iota(jnp.int32, (lanes, lanes), 1)
    before = (j_col < j_row).astype(F32).astype(BF16)
    ones = jnp.ones((codes[0].shape[1], lanes), BF16)
    base = jnp.zeros((1, lanes), F32)
    listed = [jnp.zeros((1, lanes), F32)] * rows
    j_wide = lax.broadcasted_iota(jnp.int32, (lanes, codes[0].shape[1]), 0)
    for source, row in enumerate(codes):
        local = row.astype(jnp.int32) - 1 - 8 * first
        hit = ((local == j_wide) & (j_wide < slots)).astype(F32).astype(BF16)
        times = dot(hit, ones)
        active = times > 0.0
        flag = active.astype(F32)
        position = dot(before, flag.astype(BF16)) + base
        position = jnp.where(active, position, -1.0).astype(jnp.int32)
        value = (source * lanes + j_row).astype(F32) + 1024.0 * times
        for g in range(rows):
            here = jnp.where(position == j_col + g * lanes, value, 0.0)
            listed[g] = listed[g] + jnp.sum(here, axis=0, keepdims=True)
        base = base + jnp.sum(flag, axis=0, keepdims=True)
    fill = [jnp.zeros((1, lanes), F32)] * (7 - rows)
    return jnp.concatenate(listed + [base] + fill, 0).astype(jnp.int32)


def profile(s):
    s = jnp.minimum(jnp.maximum(s, TINY), SCALE * SCALE)
    r = pl.reciprocal(lax.rsqrt(s), approx=True)
    u = SCALE - r
    u2 = u * u
    u3 = u2 * u
    u4 = u2 * u2
    return u4 * (SCALE / 4 + r), u3


def split_small(x):
    high = x.astype(BF16)
    return high, (x - high.astype(F32)).astype(F8)


def run_pairs(list_ref, count, table_ref, tables, total_ref, work):
    nodes_ref, sens_ref, small_ref, inverse_ref = tables
    s0, s1, f0, f1, g0, g1 = work

    def item(k):
        value = list_ref[k // 128, k % 128]
        code = value % 1024
        tile = (code // 128) * 8 + code % 8
        block = (code % 128) // 8
        return tile, block, (value // 1024).astype(F32), code // 128

    def items(p):
        p = jnp.maximum(p, 0)
        return item(2 * p), item(2 * p + 1)

    lane = lax.broadcasted_iota(jnp.int32, (512, 64), 1)

    def distances(p, out):
        (t1, b1, _, _), (t2, b2, _, _) = items(p)
        zero = jnp.zeros((32, 128), BF16)
        rhs = jnp.concatenate(
            [jnp.concatenate([table_ref[b1], zero], 1), jnp.concatenate([zero, table_ref[b2]], 1)], 0
        )
        lhs = jnp.where(lane < 32, nodes_ref[t1], nodes_ref[t2])
        out[...] = dot(lhs, rhs)

    def profiles(s_ref, out, low):
        for k in range(0, 512, 64):
            rows = slice(k, k + 64)
            kernel, slope = profile(s_ref[rows])
            out[0, rows], low[0, rows] = split_small(kernel)
            out[1, rows], low[1, rows] = split_small(slope)

    def sums(p, f_ref, g_ref):
        (t1, b1, m1, o1), (t2, b2, m2, o2) = items(p)
        left, right = sens_ref[t1], sens_ref[t2]
        kernel = dot(jnp.concatenate([left[0:16], right[0:16]], 0), f_ref[0])
        small = jnp.concatenate([small_ref[t1], small_ref[t2]], 0)
        kernel_low = dot(small, g_ref[0])
        slope = dot(jnp.concatenate([left, right], 0), f_ref[1])
        slope_low = dot(small, g_ref[1])
        w1 = (m1 * inverse_ref[o1])[0:1]
        w2 = (m2 * inverse_ref[o2])[0:1]
        total_ref[b1, 0:8] += m1 * kernel[0:8, :128]
        total_ref[b1, 8:32] += m1 * slope[0:24, :128]
        total_ref[b1, 32:48] += w1 * kernel_low[0:16, :128]
        total_ref[b1, 48:72] += w1 * slope_low[0:24, :128]
        total_ref[b2, 0:8] += m2 * kernel[16:24, 128:]
        total_ref[b2, 8:32] += m2 * slope[32:56, 128:]
        total_ref[b2, 32:48] += w2 * kernel_low[32:48, 128:]
        total_ref[b2, 48:72] += w2 * slope_low[32:56, 128:]

    units = (count + 3) // 4

    @pl.when(units > 0)
    def _():
        distances(0, s0)
        f1[...] = jnp.zeros_like(f1)
        g1[...] = jnp.zeros_like(g1)

        def unit(j):
            p = 2 * j
            sums(p - 1, f1, g1)
            distances(p + 1, s1)
            profiles(s0, f0, g0)
            sums(p, f0, g0)
            distances(p + 2, s0)
            profiles(s1, f1, g1)

        def long_step(j, carry):
            for k in range(4):
                unit(4 * j + k)
            return carry

        def short_step(j, carry):
            unit(j)
            return carry

        lax.fori_loop(0, units // 4, long_step, 0)
        lax.fori_loop(units // 4 * 4, units, short_step, 0)
        sums(2 * units - 1, f1, g1)


def own_kernel(packed_ref, centres_ref, first_ref, total_ref, table_ref, *scratch):
    *tables, rows_ref, list_vmem, list_smem, sem = scratch[:8]
    work = scratch[8:]
    blocks = table_ref.shape[0]
    for block in range(blocks):
        prepare_centres(centres_ref[:, block * 128 : (block + 1) * 128], table_ref, block)
    list_vmem[...] = list_pairs([packed_ref[6, 0:1, 0:256]], first_ref[0], blocks, 2)
    copy = pltpu.make_async_copy(list_vmem, list_smem, sem)
    copy.start()
    total_ref[...] = jnp.zeros_like(total_ref)
    prepare_source(packed_ref, *tables, rows_ref.at[0], 0)
    copy.wait()
    run_pairs(list_smem, list_smem[2, 0], table_ref, tables, total_ref, work)


def near_kernel(p0, p1, p2, p3, centres_ref, weights_ref, first_ref, before_ref, table_ref, *rest):
    grad_w, grad_c, total_ref, *tables = rest[:7]
    rows_ref, list_vmem, list_smem, sem = rest[7:11]
    work = rest[11:]
    packed = (p0, p1, p2, p3)
    blocks = table_ref.shape[0]
    list_vmem[...] = list_pairs([p[6, 0:1, 0:256] for p in packed], first_ref[0], blocks, 5)
    copy = pltpu.make_async_copy(list_vmem, list_smem, sem)
    copy.start()
    total_ref[...] = before_ref[...]
    for source, ref in enumerate(packed):
        prepare_source(ref, *tables, rows_ref.at[source], source)
    copy.wait()
    run_pairs(list_smem, list_smem[5, 0], table_ref, tables, total_ref, work)
    for block in range(blocks):
        total = total_ref[block]
        here = slice(block * 128, (block + 1) * 128)
        grad_w[:, here] = (4.0 / SCALE**5) * (total[0:3] + total[3:6] + (total[32:35] + total[44:47]))
        low = total[48:60] + total[60:72]
        plain = total[8:11] + total[11:14] + low[0:3]
        moments = total[14:23] + total[23:32] + low[3:12]
        a = (centres_ref[:, here] - MIDDLE) * (SCALE / 2)
        w = weights_ref[:, here] * (-10.0 / SCALE**4)
        for j in range(3):
            terms = w * (a[j : j + 1] * plain - moments[3 * j : 3 * j + 3])
            grad_c[j : j + 1, here] = jnp.sum(terms, axis=0, keepdims=True)


def body(node_coords, node_sens, centre_coords, centre_weights, pair_list, pair_count):
    device = lax.axis_index("tile")
    tiles, _, nodes = node_coords.shape
    slots = pair_list.shape[1]
    blocks = centre_coords.shape[1] // CENTRE_BLOCK
    code = pair_list[0] * 8 + pair_list[1] + 1
    code = jnp.where(jnp.arange(slots) < pair_count[0], code, 0).astype(F32)
    code = jnp.pad(code[None, None], ((0, 0), (0, tiles - 1), (0, nodes - slots)))
    packed = jnp.concatenate([node_coords.transpose(1, 0, 2), node_sens.transpose(1, 0, 2), code], 0)
    near = [swap(packed, "tile", by, phase) for by in (1, 2) for phase in (0, 1)]
    first = (device * blocks).astype(jnp.int32).reshape(1)

    vmem = pl.BlockSpec(memory_space=pltpu.VMEM)
    smem = pl.BlockSpec(memory_space=pltpu.SMEM)

    def scratch(count):
        return [
            pltpu.VMEM((count, nodes, 64), BF16),
            pltpu.VMEM((count, 32, nodes), BF16),
            pltpu.VMEM((count, 32, nodes), F8),
            pltpu.VMEM((count // 8, 8, 128), F32),
            pltpu.VMEM((count // 8, nodes // 128, 64 * 8, 128), F32),
            pltpu.VMEM((8, 128), jnp.int32),
            pltpu.SMEM((8, 128), jnp.int32),
            pltpu.SemaphoreType.DMA,
            pltpu.VMEM((nodes, 256), F32),
            pltpu.VMEM((nodes, 256), F32),
            pltpu.VMEM((2, nodes, 256), BF16),
            pltpu.VMEM((2, nodes, 256), BF16),
            pltpu.VMEM((2, nodes, 256), F8),
            pltpu.VMEM((2, nodes, 256), F8),
        ]

    params = pltpu.CompilerParams(vmem_limit_bytes=40 << 20)
    total_type = jax.ShapeDtypeStruct((blocks, 72, 128), F32)
    own, table = pl.pallas_call(
        own_kernel,
        out_shape=(total_type, jax.ShapeDtypeStruct((blocks, 32, 128), BF16)),
        in_specs=[vmem, vmem, smem],
        out_specs=(vmem, vmem),
        scratch_shapes=scratch(tiles),
        compiler_params=params,
        cost_estimate=pl.CostEstimate(flops=10**9, bytes_accessed=10**6, transcendentals=0),
        name="own_pairs",
    )(packed, centre_coords, first)
    grads = jax.ShapeDtypeStruct(centre_coords.shape, F32)
    return pl.pallas_call(
        near_kernel,
        out_shape=(grads, grads),
        in_specs=[vmem] * 6 + [smem] + [vmem] * 2,
        out_specs=(vmem, vmem),
        scratch_shapes=[pltpu.VMEM((blocks, 72, 128), F32)] + scratch(4 * tiles),
        compiler_params=params,
        name="near_pairs",
    )(*near, centre_coords, centre_weights, first, own, table)


def solution(mesh):
    return jax.shard_map(
        body,
        mesh=mesh,
        in_specs=(
            P(("case", "tile"), None, None),
            P(("case", "tile"), None, None),
            P(None, ("case", "tile")),
            P(None, ("case", "tile")),
            P(None, ("case", "tile")),
            P(("case", "tile")),
        ),
        out_specs=(P(None, ("case", "tile")), P(None, ("case", "tile"))),
        check_vma=False,
    )
```

```python
import functools

import jax
import jax.numpy as jnp
from jax import lax
from jax.experimental import pallas as pl
from jax.experimental.pallas import tpu as pltpu
from jax.sharding import PartitionSpec as P

CENTRE_BLOCK = 128
REACH = 2
MIDDLE = 1.4
SCALE = 8.0
TINY = 1e-30

F32 = jnp.float32
BF16 = jnp.bfloat16
F8 = jnp.float8_e4m3fn


def swap(array, axis, by, phase):
    devices = lax.axis_size(axis)
    pairs = []
    for i in range(devices - by):
        if (i // by) % 2 == phase:
            pairs += [(i, i + by), (i + by, i)]
    return lax.ppermute(array, axis, pairs)


def dot(a, b):
    return lax.dot_general(a, b, (((1,), (0,)), ((), ())), preferred_element_type=F32)


def split2(x):
    high = x.astype(BF16)
    return high, (x - high.astype(F32)).astype(BF16)


def split3(x):
    one = x.astype(BF16).astype(F32)
    rest = x - one
    two = rest.astype(BF16).astype(F32)
    return one, two, rest - two


def prepare_centres(centres, table_ref, block):
    a = (centres - MIDDLE) * (SCALE / 2)
    norm = jnp.sum(a * a, axis=0, keepdims=True)
    a1, a2, a3 = split3(a * -2.0)
    n1, n2, n3 = split3(norm)
    ones = jnp.ones((3, CENTRE_BLOCK), F32)
    zeros = jnp.zeros((2, CENTRE_BLOCK), F32)
    rows = [a1, a1, ones[:2], a2, a2, zeros, a3, a3, zeros, a1, ones[:1], n1, n2, n3, zeros[:1]]
    table_ref[block] = jnp.concatenate(rows, 0).astype(BF16)


def prepare_source(packed_ref, nodes_ref, sens_ref, small_ref, inverse_ref, rows_ref, source):
    place = [(packed_ref[j] - MIDDLE) * (SCALE / 2) for j in range(3)]
    sens = [packed_ref[3 + k] for k in range(3)]
    parts = [split3(x) for x in place]
    q1, q2, q3 = ([p[i] for p in parts] for i in range(3))
    norm = split3(place[0] * place[0] + place[1] * place[1] + place[2] * place[2])
    one = jnp.ones_like(place[0])
    zero = jnp.zeros_like(one)
    groups = one.shape[1] // 128
    empty = jnp.zeros((8, 128), F32)
    kinds = q1 + q2 + list(norm[:2]) + q3 + [norm[2], one, one, one, zero]
    moments = sens + [s * place[j] for j in range(3) for s in sens]
    halves = [split2(m) for m in moments]
    high = [h.astype(F32) for h, _ in halves]
    low = [l.astype(F32) for _, l in halves]
    kinds += high[:3] + low[:3] + high[3:] + low[3:]
    largest = functools.reduce(jnp.maximum, [jnp.abs(m) for m in moments])
    largest = jnp.maximum(jnp.max(largest, axis=1, keepdims=True), TINY)
    inverse_ref[source] = jnp.broadcast_to(largest * (1.0 / 128.0), (8, 128))
    factor = 128.0 / largest
    small = [m * factor for m in moments]
    upper = [m.astype(F8).astype(F32) for m in small]
    kinds += upper + [m - h for m, h in zip(small, upper)]
    for kind, value in enumerate(kinds):
        for g in range(groups):
            rows_ref[g, 8 * kind : 8 * kind + 8] = value[:, g * 128 : (g + 1) * 128]
    for t in range(8):
        for g in range(groups):
            lanes = slice(g * 128, (g + 1) * 128)
            rows = rows_ref[g, pl.ds(t, 16, stride=8), :]
            first, second = rows[0:8], rows[8:16]
            rows = jnp.concatenate([first, first, first, second], 0).astype(BF16)
            nodes_ref[8 * source + t, lanes] = jnp.concatenate([rows, rows], 0).T
            rows = jnp.concatenate([rows_ref[g, pl.ds(128 + t, 24, stride=8), :], empty], 0)
            sens_ref[8 * source + t, :, lanes] = rows.astype(BF16)
            rows = jnp.concatenate([rows_ref[g, pl.ds(320 + t, 24, stride=8), :], empty], 0)
            small_ref[8 * source + t, :, lanes] = rows.astype(F8)


def list_pairs(codes, first, blocks, rows):
    slots = 8 * blocks
    lanes = CENTRE_BLOCK
    j_row = lax.broadcasted_iota(jnp.int32, (lanes, lanes), 0)
    j_col = lax.broadcasted_iota(jnp.int32, (lanes, lanes), 1)
    before = (j_col < j_row).astype(F32).astype(BF16)
    ones = jnp.ones((codes[0].shape[1], lanes), BF16)
    base = jnp.zeros((1, lanes), F32)
    listed = [jnp.zeros((1, lanes), F32)] * rows
    j_wide = lax.broadcasted_iota(jnp.int32, (lanes, codes[0].shape[1]), 0)
    for source, row in enumerate(codes):
        local = row.astype(jnp.int32) - 1 - 8 * first
        hit = ((local == j_wide) & (j_wide < slots)).astype(F32).astype(BF16)
        times = dot(hit, ones)
        active = times > 0.0
        flag = active.astype(F32)
        position = dot(before, flag.astype(BF16)) + base
        position = jnp.where(active, position, -1.0).astype(jnp.int32)
        value = (source * lanes + j_row).astype(F32) + 1024.0 * times
        for g in range(rows):
            here = jnp.where(position == j_col + g * lanes, value, 0.0)
            listed[g] = listed[g] + jnp.sum(here, axis=0, keepdims=True)
        base = base + jnp.sum(flag, axis=0, keepdims=True)
    fill = [jnp.zeros((1, lanes), F32)] * (7 - rows)
    return jnp.concatenate(listed + [base] + fill, 0).astype(jnp.int32)


def profile(s):
    s = jnp.minimum(jnp.maximum(s, TINY), SCALE * SCALE)
    r = pl.reciprocal(lax.rsqrt(s), approx=True)
    u = SCALE - r
    u2 = u * u
    u3 = u2 * u
    u4 = u2 * u2
    return u4 * (SCALE / 4 + r), u3


def split_small(x):
    high = x.astype(BF16)
    return high, (x - high.astype(F32)).astype(F8)


def run_pairs(list_ref, count, table_ref, tables, total_ref, work):
    nodes_ref, sens_ref, small_ref, inverse_ref = tables
    s0, s1, f0, f1, g0, g1 = work

    def item(k):
        value = list_ref[k >> 7, k & 127]
        code = value & 1023
        tile = (code >> 7) * 8 + (code & 7)
        block = (code & 127) >> 3
        return tile, block, (value >> 10).astype(F32)

    def items(p):
        p = jnp.maximum(p, 0)
        return item(2 * p), item(2 * p + 1)

    lane = lax.broadcasted_iota(jnp.int32, (512, 64), 1)

    def distances(p, out):
        (t1, b1, _), (t2, b2, _) = items(p)
        zero = jnp.zeros((32, 128), BF16)
        rhs = jnp.concatenate(
            [jnp.concatenate([table_ref[b1], zero], 1), jnp.concatenate([zero, table_ref[b2]], 1)], 0
        )
        lhs = jnp.where(lane < 32, nodes_ref[t1], nodes_ref[t2])
        out[...] = dot(lhs, rhs)

    def profiles(s_ref, out, low):
        for k in range(0, 512, 64):
            rows = slice(k, k + 64)
            kernel, slope = profile(s_ref[rows])
            out[0, rows], low[0, rows] = split_small(kernel)
            out[1, rows], low[1, rows] = split_small(slope)

    def sums(p, f_ref, g_ref):
        (t1, b1, m1), (t2, b2, m2) = items(p)
        left, right = sens_ref[t1], sens_ref[t2]
        kernel = dot(jnp.concatenate([left[0:16], right[0:16]], 0), f_ref[0])
        small = jnp.concatenate([small_ref[t1], small_ref[t2]], 0)
        kernel_low = dot(small, g_ref[0])
        slope = dot(jnp.concatenate([left, right], 0), f_ref[1])
        slope_low = dot(small, g_ref[1])
        w1 = m1 * inverse_ref[t1 >> 3, pl.ds(t1 & 7, 1), :]
        w2 = m2 * inverse_ref[t2 >> 3, pl.ds(t2 & 7, 1), :]
        total_ref[b1, 0:8] += m1 * kernel[0:8, :128]
        total_ref[b1, 8:32] += m1 * slope[0:24, :128]
        total_ref[b1, 32:48] += w1 * kernel_low[0:16, :128]
        total_ref[b1, 48:72] += w1 * slope_low[0:24, :128]
        total_ref[b2, 0:8] += m2 * kernel[16:24, 128:]
        total_ref[b2, 8:32] += m2 * slope[32:56, 128:]
        total_ref[b2, 32:48] += w2 * kernel_low[32:48, 128:]
        total_ref[b2, 48:72] += w2 * slope_low[32:56, 128:]

    units = (count + 3) // 4

    @pl.when(units > 0)
    def _():
        distances(0, s0)
        f1[...] = jnp.zeros_like(f1)
        g1[...] = jnp.zeros_like(g1)

        def unit(j):
            p = 2 * j
            sums(p - 1, f1, g1)
            distances(p + 1, s1)
            profiles(s0, f0, g0)
            sums(p, f0, g0)
            distances(p + 2, s0)
            profiles(s1, f1, g1)

        def long_step(j, carry):
            for k in range(4):
                unit(4 * j + k)
            return carry

        def short_step(j, carry):
            unit(j)
            return carry

        lax.fori_loop(0, units // 4, long_step, 0)
        lax.fori_loop(units // 4 * 4, units, short_step, 0)
        sums(2 * units - 1, f1, g1)


def own_kernel(packed_ref, centres_ref, first_ref, total_ref, table_ref, *scratch):
    *tables, rows_ref, list_vmem, list_smem, sem = scratch[:8]
    work = scratch[8:]
    blocks = table_ref.shape[0]
    for block in range(blocks):
        prepare_centres(centres_ref[:, block * 128 : (block + 1) * 128], table_ref, block)
    list_vmem[...] = list_pairs([packed_ref[6, 0:1, 0:256]], first_ref[0], blocks, 2)
    copy = pltpu.make_async_copy(list_vmem, list_smem, sem)
    copy.start()
    total_ref[...] = jnp.zeros_like(total_ref)
    prepare_source(packed_ref, *tables, rows_ref.at[0], 0)
    copy.wait()
    run_pairs(list_smem, list_smem[2, 0], table_ref, tables, total_ref, work)


def near_kernel(p0, p1, p2, p3, centres_ref, weights_ref, first_ref, before_ref, table_ref, *rest):
    grad_w, grad_c, total_ref, *tables = rest[:7]
    rows_ref, list_vmem, list_smem, sem = rest[7:11]
    work = rest[11:]
    packed = (p0, p1, p2, p3)
    blocks = table_ref.shape[0]
    list_vmem[...] = list_pairs([p[6, 0:1, 0:256] for p in packed], first_ref[0], blocks, 5)
    copy = pltpu.make_async_copy(list_vmem, list_smem, sem)
    copy.start()
    total_ref[...] = before_ref[...]
    for source, ref in enumerate(packed):
        prepare_source(ref, *tables, rows_ref.at[source], source)
    copy.wait()
    run_pairs(list_smem, list_smem[5, 0], table_ref, tables, total_ref, work)
    for block in range(blocks):
        total = total_ref[block]
        here = slice(block * 128, (block + 1) * 128)
        grad_w[:, here] = (4.0 / SCALE**5) * (total[0:3] + total[3:6] + (total[32:35] + total[44:47]))
        low = total[48:60] + total[60:72]
        plain = total[8:11] + total[11:14] + low[0:3]
        moments = total[14:23] + total[23:32] + low[3:12]
        a = (centres_ref[:, here] - MIDDLE) * (SCALE / 2)
        w = weights_ref[:, here] * (-10.0 / SCALE**4)
        for j in range(3):
            terms = w * (a[j : j + 1] * plain - moments[3 * j : 3 * j + 3])
            grad_c[j : j + 1, here] = jnp.sum(terms, axis=0, keepdims=True)


def body(node_coords, node_sens, centre_coords, centre_weights, pair_list, pair_count):
    device = lax.axis_index("tile")
    tiles, _, nodes = node_coords.shape
    slots = pair_list.shape[1]
    blocks = centre_coords.shape[1] // CENTRE_BLOCK
    code = pair_list[0] * 8 + pair_list[1] + 1
    code = jnp.where(jnp.arange(slots) < pair_count[0], code, 0).astype(F32)
    code = jnp.pad(code[None, None], ((0, 0), (0, tiles - 1), (0, nodes - slots)))
    packed = jnp.concatenate([node_coords.transpose(1, 0, 2), node_sens.transpose(1, 0, 2), code], 0)
    near = [swap(packed, "tile", by, phase) for by in (1, 2) for phase in (0, 1)]
    first = (device * blocks).astype(jnp.int32).reshape(1)

    vmem = pl.BlockSpec(memory_space=pltpu.VMEM)
    smem = pl.BlockSpec(memory_space=pltpu.SMEM)

    def scratch(count):
        return [
            pltpu.VMEM((count, nodes, 64), BF16),
            pltpu.VMEM((count, 32, nodes), BF16),
            pltpu.VMEM((count, 32, nodes), F8),
            pltpu.VMEM((count // 8, 8, 128), F32),
            pltpu.VMEM((count // 8, nodes // 128, 64 * 8, 128), F32),
            pltpu.VMEM((8, 128), jnp.int32),
            pltpu.SMEM((8, 128), jnp.int32),
            pltpu.SemaphoreType.DMA,
            pltpu.VMEM((nodes, 256), F32),
            pltpu.VMEM((nodes, 256), F32),
            pltpu.VMEM((2, nodes, 256), BF16),
            pltpu.VMEM((2, nodes, 256), BF16),
            pltpu.VMEM((2, nodes, 256), F8),
            pltpu.VMEM((2, nodes, 256), F8),
        ]

    params = pltpu.CompilerParams(vmem_limit_bytes=40 << 20)
    total_type = jax.ShapeDtypeStruct((blocks, 72, 128), F32)
    own, table = pl.pallas_call(
        own_kernel,
        out_shape=(total_type, jax.ShapeDtypeStruct((blocks, 32, 128), BF16)),
        in_specs=[vmem, vmem, smem],
        out_specs=(vmem, vmem),
        scratch_shapes=scratch(tiles),
        compiler_params=params,
        cost_estimate=pl.CostEstimate(flops=10**9, bytes_accessed=10**6, transcendentals=0),
        name="own_pairs",
    )(packed, centre_coords, first)
    grads = jax.ShapeDtypeStruct(centre_coords.shape, F32)
    return pl.pallas_call(
        near_kernel,
        out_shape=(grads, grads),
        in_specs=[vmem] * 6 + [smem] + [vmem] * 2,
        out_specs=(vmem, vmem),
        scratch_shapes=[pltpu.VMEM((blocks, 72, 128), F32)] + scratch(4 * tiles),
        compiler_params=params,
        name="near_pairs",
    )(*near, centre_coords, centre_weights, first, own, table)


def solution(mesh):
    return jax.shard_map(
        body,
        mesh=mesh,
        in_specs=(
            P(("case", "tile"), None, None),
            P(("case", "tile"), None, None),
            P(None, ("case", "tile")),
            P(None, ("case", "tile")),
            P(None, ("case", "tile")),
            P(("case", "tile")),
        ),
        out_specs=(P(None, ("case", "tile")), P(None, ("case", "tile"))),
        check_vma=False,
    )
```

```python
import functools

import jax
import jax.numpy as jnp
from jax import lax
from jax.experimental import pallas as pl
from jax.experimental.pallas import tpu as pltpu
from jax.sharding import PartitionSpec as P

CENTRE_BLOCK = 128
REACH = 2
MIDDLE = 1.4
SCALE = 8.0
TINY = 1e-30

F32 = jnp.float32
BF16 = jnp.bfloat16
F8 = jnp.float8_e4m3fn


def swap(array, axis, by, phase):
    devices = lax.axis_size(axis)
    pairs = []
    for i in range(devices - by):
        if (i // by) % 2 == phase:
            pairs += [(i, i + by), (i + by, i)]
    return lax.ppermute(array, axis, pairs)


def dot(a, b):
    return lax.dot_general(a, b, (((1,), (0,)), ((), ())), preferred_element_type=F32)


def split2(x):
    high = x.astype(BF16)
    return high, (x - high.astype(F32)).astype(BF16)


def split3(x):
    one = x.astype(BF16).astype(F32)
    rest = x - one
    two = rest.astype(BF16).astype(F32)
    return one, two, rest - two


def prepare_centres(centres, table_ref, block):
    a = (centres - MIDDLE) * (SCALE / 2)
    norm = jnp.sum(a * a, axis=0, keepdims=True)
    a1, a2, a3 = split3(a * -2.0)
    n1, n2, n3 = split3(norm)
    ones = jnp.ones((3, CENTRE_BLOCK), F32)
    zeros = jnp.zeros((2, CENTRE_BLOCK), F32)
    rows = [a1, a1, ones[:2], a2, a2, zeros, a3, a3, zeros, a1, ones[:1], n1, n2, n3, zeros[:1]]
    table_ref[block] = jnp.concatenate(rows, 0).astype(BF16)


def prepare_source(packed_ref, nodes_ref, sens_ref, small_ref, inverse_ref, rows_ref, source):
    place = [(packed_ref[j] - MIDDLE) * (SCALE / 2) for j in range(3)]
    sens = [packed_ref[3 + k] for k in range(3)]
    parts = [split3(x) for x in place]
    q1, q2, q3 = ([p[i] for p in parts] for i in range(3))
    norm = split3(place[0] * place[0] + place[1] * place[1] + place[2] * place[2])
    one = jnp.ones_like(place[0])
    zero = jnp.zeros_like(one)
    groups = one.shape[1] // 128
    empty = jnp.zeros((8, 128), F32)
    kinds = q1 + q2 + list(norm[:2]) + q3 + [norm[2], one, one, one, zero]
    moments = sens + [s * place[j] for j in range(3) for s in sens]
    halves = [split2(m) for m in moments]
    high = [h.astype(F32) for h, _ in halves]
    low = [l.astype(F32) for _, l in halves]
    kinds += high[:3] + low[:3] + high[3:] + low[3:]
    largest = functools.reduce(jnp.maximum, [jnp.abs(m) for m in moments])
    largest = jnp.maximum(jnp.max(largest, axis=1, keepdims=True), TINY)
    inverse_ref[source] = jnp.broadcast_to(largest * (1.0 / 128.0), (8, 128))
    factor = 128.0 / largest
    small = [m * factor for m in moments]
    upper = [m.astype(F8).astype(F32) for m in small]
    kinds += upper + [m - h for m, h in zip(small, upper)]
    for kind, value in enumerate(kinds):
        for g in range(groups):
            rows_ref[g, 8 * kind : 8 * kind + 8] = value[:, g * 128 : (g + 1) * 128]
    for t in range(8):
        for g in range(groups):
            lanes = slice(g * 128, (g + 1) * 128)
            rows = rows_ref[g, pl.ds(t, 16, stride=8), :]
            first, second = rows[0:8], rows[8:16]
            rows = jnp.concatenate([first, first, first, second], 0).astype(BF16)
            nodes_ref[8 * source + t, lanes] = jnp.concatenate([rows, rows], 0).T
            rows = jnp.concatenate([rows_ref[g, pl.ds(128 + t, 24, stride=8), :], empty], 0)
            sens_ref[8 * source + t, :, lanes] = rows.astype(BF16)
            rows = jnp.concatenate([rows_ref[g, pl.ds(320 + t, 24, stride=8), :], empty], 0)
            small_ref[8 * source + t, :, lanes] = rows.astype(F8)


def list_pairs(codes, first, blocks, rows):
    slots = 8 * blocks
    lanes = CENTRE_BLOCK
    j_row = lax.broadcasted_iota(jnp.int32, (lanes, lanes), 0)
    j_col = lax.broadcasted_iota(jnp.int32, (lanes, lanes), 1)
    before = (j_col < j_row).astype(F32).astype(BF16)
    ones = jnp.ones((codes[0].shape[1], lanes), BF16)
    base = jnp.zeros((1, lanes), F32)
    listed = [jnp.zeros((1, lanes), F32)] * rows
    j_wide = lax.broadcasted_iota(jnp.int32, (lanes, codes[0].shape[1]), 0)
    for source, row in enumerate(codes):
        local = row.astype(jnp.int32) - 1 - 8 * first
        hit = ((local == j_wide) & (j_wide < slots)).astype(F32).astype(BF16)
        times = dot(hit, ones)
        active = times > 0.0
        flag = active.astype(F32)
        position = dot(before, flag.astype(BF16)) + base
        position = jnp.where(active, position, -1.0).astype(jnp.int32)
        value = (source * lanes + j_row).astype(F32) + 1024.0 * times
        for g in range(rows):
            here = jnp.where(position == j_col + g * lanes, value, 0.0)
            listed[g] = listed[g] + jnp.sum(here, axis=0, keepdims=True)
        base = base + jnp.sum(flag, axis=0, keepdims=True)
    fill = [jnp.zeros((1, lanes), F32)] * (7 - rows)
    return jnp.concatenate(listed + [base] + fill, 0).astype(jnp.int32)


def profile(s):
    s = jnp.minimum(jnp.maximum(s, TINY), SCALE * SCALE)
    r = pl.reciprocal(lax.rsqrt(s), approx=True)
    u = SCALE - r
    u2 = u * u
    u3 = u2 * u
    u4 = u2 * u2
    return u4 * (SCALE / 4 + r), u3


def split_small(x):
    high = x.astype(BF16)
    return high, (x - high.astype(F32)).astype(F8)


def run_pairs(list_ref, count, table_ref, tables, total_ref, work):
    nodes_ref, sens_ref, small_ref, inverse_ref = tables
    s0, s1, f0, f1, g0, g1 = work

    def item(k):
        value = list_ref[k >> 7, k & 127]
        code = value & 1023
        tile = (code >> 7) * 8 + (code & 7)
        block = (code & 127) >> 3
        return tile, block, (value >> 10).astype(F32)

    def items(p):
        p = jnp.maximum(p, 0)
        return item(2 * p), item(2 * p + 1)

    lane = lax.broadcasted_iota(jnp.int32, (512, 64), 1)

    def distances(p, out):
        (t1, b1, _), (t2, b2, _) = items(p)
        zero = jnp.zeros((32, 128), BF16)
        rhs = jnp.concatenate(
            [jnp.concatenate([table_ref[b1], zero], 1), jnp.concatenate([zero, table_ref[b2]], 1)], 0
        )
        lhs = jnp.where(lane < 32, nodes_ref[t1], nodes_ref[t2])
        out[...] = dot(lhs, rhs)

    def profiles(s_ref, out, low):
        for k in range(0, 512, 64):
            rows = slice(k, k + 64)
            kernel, slope = profile(s_ref[rows])
            out[0, rows], low[0, rows] = split_small(kernel)
            out[1, rows], low[1, rows] = split_small(slope)

    def sums(p, f_ref, g_ref):
        (t1, b1, m1), (t2, b2, m2) = items(p)
        left, right = sens_ref[t1], sens_ref[t2]
        kernel = dot(jnp.concatenate([left[0:16], right[0:16]], 0), f_ref[0])
        small = jnp.concatenate([small_ref[t1], small_ref[t2]], 0)
        kernel_low = dot(small, g_ref[0])
        slope = dot(jnp.concatenate([left, right], 0), f_ref[1])
        slope_low = dot(small, g_ref[1])
        w1 = m1 * inverse_ref[t1 >> 3, pl.ds(t1 & 7, 1), :]
        w2 = m2 * inverse_ref[t2 >> 3, pl.ds(t2 & 7, 1), :]
        total_ref[b1, 0:8] += m1 * kernel[0:8, :128]
        total_ref[b1, 8:32] += m1 * slope[0:24, :128]
        total_ref[b1, 32:48] += w1 * kernel_low[0:16, :128]
        total_ref[b1, 48:72] += w1 * slope_low[0:24, :128]
        total_ref[b2, 0:8] += m2 * kernel[16:24, 128:]
        total_ref[b2, 8:32] += m2 * slope[32:56, 128:]
        total_ref[b2, 32:48] += w2 * kernel_low[32:48, 128:]
        total_ref[b2, 48:72] += w2 * slope_low[32:56, 128:]

    units = (count + 3) // 4

    @pl.when(units > 0)
    def _():
        distances(0, s0)
        f1[...] = jnp.zeros_like(f1)
        g1[...] = jnp.zeros_like(g1)

        def unit(j):
            p = 2 * j
            sums(p - 1, f1, g1)
            distances(p + 1, s1)
            profiles(s0, f0, g0)
            sums(p, f0, g0)
            distances(p + 2, s0)
            profiles(s1, f1, g1)

        def long_step(j, carry):
            for k in range(4):
                unit(4 * j + k)
            return carry

        def short_step(j, carry):
            unit(j)
            return carry

        lax.fori_loop(0, units // 4, long_step, 0)
        lax.fori_loop(units // 4 * 4, units, short_step, 0)
        sums(2 * units - 1, f1, g1)


def own_kernel(packed_ref, centres_ref, first_ref, total_ref, table_ref, *scratch):
    *tables, rows_ref, list_vmem, list_smem, sem = scratch[:8]
    work = scratch[8:]
    blocks = table_ref.shape[0]
    for block in range(blocks):
        prepare_centres(centres_ref[:, block * 128 : (block + 1) * 128], table_ref, block)
    list_vmem[...] = list_pairs([packed_ref[6, 0:1, 0:256]], first_ref[0], blocks, 2)
    copy = pltpu.make_async_copy(list_vmem, list_smem, sem)
    copy.start()
    total_ref[...] = jnp.zeros_like(total_ref)
    prepare_source(packed_ref, *tables, rows_ref.at[0], 0)
    copy.wait()
    run_pairs(list_smem, list_smem[2, 0], table_ref, tables, total_ref, work)


def near_kernel(p0, p1, p2, p3, centres_ref, weights_ref, first_ref, before_ref, table_ref, *rest):
    grad_w, grad_c, total_ref, *tables = rest[:7]
    rows_ref, list_vmem, list_smem, sem = rest[7:11]
    work = rest[11:]
    packed = (p0, p1, p2, p3)
    blocks = table_ref.shape[0]
    list_vmem[...] = list_pairs([p[6, 0:1, 0:256] for p in packed], first_ref[0], blocks, 5)
    copy = pltpu.make_async_copy(list_vmem, list_smem, sem)
    copy.start()
    total_ref[...] = before_ref[...]
    for source, ref in enumerate(packed):
        prepare_source(ref, *tables, rows_ref.at[source], source)
    copy.wait()
    run_pairs(list_smem, list_smem[5, 0], table_ref, tables, total_ref, work)
    for block in range(blocks):
        total = total_ref[block]
        here = slice(block * 128, (block + 1) * 128)
        grad_w[:, here] = (4.0 / SCALE**5) * (total[0:3] + total[3:6] + (total[32:35] + total[44:47]))
        low = total[48:60] + total[60:72]
        plain = total[8:11] + total[11:14] + low[0:3]
        moments = total[14:23] + total[23:32] + low[3:12]
        a = (centres_ref[:, here] - MIDDLE) * (SCALE / 2)
        w = weights_ref[:, here] * (-10.0 / SCALE**4)
        for j in range(3):
            terms = w * (a[j : j + 1] * plain - moments[3 * j : 3 * j + 3])
            grad_c[j : j + 1, here] = jnp.sum(terms, axis=0, keepdims=True)


def body(node_coords, node_sens, centre_coords, centre_weights, pair_list, pair_count):
    device = lax.axis_index("tile")
    tiles, _, nodes = node_coords.shape
    slots = pair_list.shape[1]
    blocks = centre_coords.shape[1] // CENTRE_BLOCK
    code = pair_list[0] * 8 + pair_list[1] + 1
    code = jnp.where(jnp.arange(slots) < pair_count[0], code, 0).astype(F32)
    code = jnp.pad(code[None, None], ((0, 0), (0, tiles - 1), (0, nodes - slots)))
    packed = jnp.concatenate([node_coords.transpose(1, 0, 2), node_sens.transpose(1, 0, 2), code], 0)
    near = [swap(packed, "tile", by, phase) for by, phase in ((2, 0), (1, 1), (2, 1), (1, 0))]
    first = (device * blocks).astype(jnp.int32).reshape(1)

    vmem = pl.BlockSpec(memory_space=pltpu.VMEM)
    smem = pl.BlockSpec(memory_space=pltpu.SMEM)

    def scratch(count):
        return [
            pltpu.VMEM((count, nodes, 64), BF16),
            pltpu.VMEM((count, 32, nodes), BF16),
            pltpu.VMEM((count, 32, nodes), F8),
            pltpu.VMEM((count // 8, 8, 128), F32),
            pltpu.VMEM((count // 8, nodes // 128, 64 * 8, 128), F32),
            pltpu.VMEM((8, 128), jnp.int32),
            pltpu.SMEM((8, 128), jnp.int32),
            pltpu.SemaphoreType.DMA,
            pltpu.VMEM((nodes, 256), F32),
            pltpu.VMEM((nodes, 256), F32),
            pltpu.VMEM((2, nodes, 256), BF16),
            pltpu.VMEM((2, nodes, 256), BF16),
            pltpu.VMEM((2, nodes, 256), F8),
            pltpu.VMEM((2, nodes, 256), F8),
        ]

    params = pltpu.CompilerParams(vmem_limit_bytes=40 << 20)
    total_type = jax.ShapeDtypeStruct((blocks, 72, 128), F32)
    own, table = pl.pallas_call(
        own_kernel,
        out_shape=(total_type, jax.ShapeDtypeStruct((blocks, 32, 128), BF16)),
        in_specs=[vmem, vmem, smem],
        out_specs=(vmem, vmem),
        scratch_shapes=scratch(tiles),
        compiler_params=params,
        cost_estimate=pl.CostEstimate(flops=10**9, bytes_accessed=10**6, transcendentals=0),
        name="own_pairs",
    )(packed, centre_coords, first)
    grads = jax.ShapeDtypeStruct(centre_coords.shape, F32)
    return pl.pallas_call(
        near_kernel,
        out_shape=(grads, grads),
        in_specs=[vmem] * 6 + [smem] + [vmem] * 2,
        out_specs=(vmem, vmem),
        scratch_shapes=[pltpu.VMEM((blocks, 72, 128), F32)] + scratch(4 * tiles),
        compiler_params=params,
        name="near_pairs",
    )(*near, centre_coords, centre_weights, first, own, table)


def solution(mesh):
    return jax.shard_map(
        body,
        mesh=mesh,
        in_specs=(
            P(("case", "tile"), None, None),
            P(("case", "tile"), None, None),
            P(None, ("case", "tile")),
            P(None, ("case", "tile")),
            P(None, ("case", "tile")),
            P(("case", "tile")),
        ),
        out_specs=(P(None, ("case", "tile")), P(None, ("case", "tile"))),
        check_vma=False,
    )
```

```python
import functools

import jax
import jax.numpy as jnp
from jax import lax
from jax.experimental import pallas as pl
from jax.experimental.pallas import tpu as pltpu
from jax.sharding import PartitionSpec as P

CENTRE_BLOCK = 128
REACH = 2
MIDDLE = 1.4
SCALE = 8.0
TINY = 1e-30

F32 = jnp.float32
BF16 = jnp.bfloat16
F8 = jnp.float8_e4m3fn


def swap(array, axis, by, phase):
    devices = lax.axis_size(axis)
    pairs = []
    for i in range(devices - by):
        if (i // by) % 2 == phase:
            pairs += [(i, i + by), (i + by, i)]
    return lax.ppermute(array, axis, pairs)


def dot(a, b):
    return lax.dot_general(a, b, (((1,), (0,)), ((), ())), preferred_element_type=F32)


def split2(x):
    high = x.astype(BF16)
    return high, (x - high.astype(F32)).astype(BF16)


def split3(x):
    one = x.astype(BF16).astype(F32)
    rest = x - one
    two = rest.astype(BF16).astype(F32)
    return one, two, rest - two


def prepare_centres(centres, table_ref, block):
    a = (centres - MIDDLE) * (SCALE / 2)
    norm = jnp.sum(a * a, axis=0, keepdims=True)
    a1, a2, a3 = split3(a * -2.0)
    n1, n2, n3 = split3(norm)
    ones = jnp.ones((3, CENTRE_BLOCK), F32)
    zeros = jnp.zeros((2, CENTRE_BLOCK), F32)
    rows = [a1, a1, ones[:2], a2, a2, zeros, a3, a3, zeros, a1, ones[:1], n1, n2, n3, zeros[:1]]
    table_ref[block] = jnp.concatenate(rows, 0).astype(BF16)


def prepare_source(packed_ref, nodes_ref, sens_ref, small_ref, inverse_ref, rows_ref, source):
    place = [(packed_ref[j] - MIDDLE) * (SCALE / 2) for j in range(3)]
    sens = [packed_ref[3 + k] for k in range(3)]
    parts = [split3(x) for x in place]
    q1, q2, q3 = ([p[i] for p in parts] for i in range(3))
    norm = split3(place[0] * place[0] + place[1] * place[1] + place[2] * place[2])
    one = jnp.ones_like(place[0])
    zero = jnp.zeros_like(one)
    groups = one.shape[1] // 128
    empty = jnp.zeros((8, 128), F32)
    kinds = q1 + q2 + list(norm[:2]) + q3 + [norm[2], one, one, one, zero]
    moments = sens + [s * place[j] for j in range(3) for s in sens]
    halves = [split2(m) for m in moments]
    high = [h.astype(F32) for h, _ in halves]
    low = [l.astype(F32) for _, l in halves]
    kinds += high[:3] + low[:3] + high[3:] + low[3:]
    largest = functools.reduce(jnp.maximum, [jnp.abs(m) for m in moments])
    largest = jnp.maximum(jnp.max(largest, axis=1, keepdims=True), TINY)
    inverse_ref[source] = jnp.broadcast_to(largest * (1.0 / 128.0), (8, 128))
    factor = 128.0 / largest
    small = [m * factor for m in moments]
    upper = [m.astype(F8).astype(F32) for m in small]
    kinds += upper + [m - h for m, h in zip(small, upper)]
    for kind, value in enumerate(kinds):
        for g in range(groups):
            rows_ref[g, 8 * kind : 8 * kind + 8] = value[:, g * 128 : (g + 1) * 128]
    for t in range(8):
        for g in range(groups):
            lanes = slice(g * 128, (g + 1) * 128)
            rows = rows_ref[g, pl.ds(t, 16, stride=8), :]
            first, second = rows[0:8], rows[8:16]
            rows = jnp.concatenate([first, first, first, second], 0).astype(BF16)
            nodes_ref[8 * source + t, lanes] = jnp.concatenate([rows, rows], 0).T
            rows = jnp.concatenate([rows_ref[g, pl.ds(128 + t, 24, stride=8), :], empty], 0)
            sens_ref[8 * source + t, :, lanes] = rows.astype(BF16)
            rows = jnp.concatenate([rows_ref[g, pl.ds(320 + t, 24, stride=8), :], empty], 0)
            small_ref[8 * source + t, :, lanes] = rows.astype(F8)


def list_pairs(codes, first, blocks, rows):
    slots = 8 * blocks
    lanes = CENTRE_BLOCK
    j_row = lax.broadcasted_iota(jnp.int32, (lanes, lanes), 0)
    j_col = lax.broadcasted_iota(jnp.int32, (lanes, lanes), 1)
    before = (j_col < j_row).astype(F32).astype(BF16)
    ones = jnp.ones((codes[0].shape[1], lanes), BF16)
    base = jnp.zeros((1, lanes), F32)
    listed = [jnp.zeros((1, lanes), F32)] * rows
    j_wide = lax.broadcasted_iota(jnp.int32, (lanes, codes[0].shape[1]), 0)
    for source, row in enumerate(codes):
        local = row.astype(jnp.int32) - 1 - 8 * first
        hit = ((local == j_wide) & (j_wide < slots)).astype(F32).astype(BF16)
        times = dot(hit, ones)
        active = times > 0.0
        flag = active.astype(F32)
        position = dot(before, flag.astype(BF16)) + base
        position = jnp.where(active, position, -1.0).astype(jnp.int32)
        value = (source * lanes + j_row).astype(F32) + 1024.0 * times
        for g in range(rows):
            here = jnp.where(position == j_col + g * lanes, value, 0.0)
            listed[g] = listed[g] + jnp.sum(here, axis=0, keepdims=True)
        base = base + jnp.sum(flag, axis=0, keepdims=True)
    fill = [jnp.zeros((1, lanes), F32)] * (7 - rows)
    return jnp.concatenate(listed + [base] + fill, 0).astype(jnp.int32)


def profile(s):
    s = jnp.minimum(jnp.maximum(s, TINY), SCALE * SCALE)
    r = pl.reciprocal(lax.rsqrt(s), approx=True)
    u = SCALE - r
    u2 = u * u
    u3 = u2 * u
    u4 = u2 * u2
    return u4 * (SCALE / 4 + r), u3


def split_small(x):
    high = x.astype(BF16)
    return high, (x - high.astype(F32)).astype(F8)


def run_pairs(list_ref, count, table_ref, tables, total_ref, work):
    nodes_ref, sens_ref, small_ref, inverse_ref = tables
    s0, s1, f0, f1, g0, g1 = work

    def item(k):
        value = list_ref[k >> 7, k & 127]
        code = value & 1023
        tile = (code >> 7) * 8 + (code & 7)
        block = (code & 127) >> 3
        return tile, block, (value >> 10).astype(F32)

    def items(p):
        p = jnp.maximum(p, 0)
        return item(2 * p), item(2 * p + 1)

    lane = lax.broadcasted_iota(jnp.int32, (512, 64), 1)

    def distances(p, out):
        (t1, b1, _), (t2, b2, _) = items(p)
        zero = jnp.zeros((32, 128), BF16)
        rhs = jnp.concatenate(
            [jnp.concatenate([table_ref[b1], zero], 1), jnp.concatenate([zero, table_ref[b2]], 1)], 0
        )
        lhs = jnp.where(lane < 32, nodes_ref[t1], nodes_ref[t2])
        out[...] = dot(lhs, rhs)

    def profiles(s_ref, out, low):
        for k in range(0, 512, 64):
            rows = slice(k, k + 64)
            kernel, slope = profile(s_ref[rows])
            out[0, rows], low[0, rows] = split_small(kernel)
            out[1, rows], low[1, rows] = split_small(slope)

    def sums(p, f_ref, g_ref):
        (t1, b1, m1), (t2, b2, m2) = items(p)
        left, right = sens_ref[t1], sens_ref[t2]
        kernel = dot(jnp.concatenate([left[0:16], right[0:16]], 0), f_ref[0])
        small = jnp.concatenate([small_ref[t1], small_ref[t2]], 0)
        kernel_low = dot(small, g_ref[0])
        slope = dot(jnp.concatenate([left, right], 0), f_ref[1])
        slope_low = dot(small, g_ref[1])
        w1 = m1 * inverse_ref[t1 >> 3, pl.ds(t1 & 7, 1), :]
        w2 = m2 * inverse_ref[t2 >> 3, pl.ds(t2 & 7, 1), :]
        total_ref[b1, 0:8] += m1 * kernel[0:8, :128]
        total_ref[b1, 8:32] += m1 * slope[0:24, :128]
        total_ref[b1, 32:48] += w1 * kernel_low[0:16, :128]
        total_ref[b1, 48:72] += w1 * slope_low[0:24, :128]
        total_ref[b2, 0:8] += m2 * kernel[16:24, 128:]
        total_ref[b2, 8:32] += m2 * slope[32:56, 128:]
        total_ref[b2, 32:48] += w2 * kernel_low[32:48, 128:]
        total_ref[b2, 48:72] += w2 * slope_low[32:56, 128:]

    units = (count + 3) // 4

    @pl.when(units > 0)
    def _():
        distances(0, s0)
        f1[...] = jnp.zeros_like(f1)
        g1[...] = jnp.zeros_like(g1)

        def unit(j):
            p = 2 * j
            sums(p - 1, f1, g1)
            distances(p + 1, s1)
            profiles(s0, f0, g0)
            sums(p, f0, g0)
            distances(p + 2, s0)
            profiles(s1, f1, g1)

        def long_step(j, carry):
            for k in range(4):
                unit(4 * j + k)
            return carry

        def short_step(j, carry):
            unit(j)
            return carry

        def double_step(j, carry):
            unit(2 * j)
            unit(2 * j + 1)
            return carry

        lax.fori_loop(0, units // 4, long_step, 0)
        lax.fori_loop(units // 4 * 2, units // 2, double_step, 0)
        lax.fori_loop(units // 2 * 2, units, short_step, 0)
        sums(2 * units - 1, f1, g1)


def own_kernel(packed_ref, centres_ref, first_ref, total_ref, table_ref, *scratch):
    *tables, rows_ref, list_vmem, list_smem, sem = scratch[:8]
    work = scratch[8:]
    blocks = table_ref.shape[0]
    for block in range(blocks):
        prepare_centres(centres_ref[:, block * 128 : (block + 1) * 128], table_ref, block)
    list_vmem[...] = list_pairs([packed_ref[6, 0:1, 0:256]], first_ref[0], blocks, 2)
    copy = pltpu.make_async_copy(list_vmem, list_smem, sem)
    copy.start()
    total_ref[...] = jnp.zeros_like(total_ref)
    prepare_source(packed_ref, *tables, rows_ref.at[0], 0)
    copy.wait()
    run_pairs(list_smem, list_smem[2, 0], table_ref, tables, total_ref, work)


def near_kernel(p0, p1, p2, p3, centres_ref, weights_ref, first_ref, before_ref, table_ref, *rest):
    grad_w, grad_c, total_ref, *tables = rest[:7]
    rows_ref, list_vmem, list_smem, sem = rest[7:11]
    work = rest[11:]
    packed = (p0, p1, p2, p3)
    blocks = table_ref.shape[0]
    list_vmem[...] = list_pairs([p[6, 0:1, 0:256] for p in packed], first_ref[0], blocks, 5)
    copy = pltpu.make_async_copy(list_vmem, list_smem, sem)
    copy.start()
    total_ref[...] = before_ref[...]
    for source, ref in enumerate(packed):
        prepare_source(ref, *tables, rows_ref.at[source], source)
    copy.wait()
    run_pairs(list_smem, list_smem[5, 0], table_ref, tables, total_ref, work)
    for block in range(blocks):
        total = total_ref[block]
        here = slice(block * 128, (block + 1) * 128)
        grad_w[:, here] = (4.0 / SCALE**5) * (total[0:3] + total[3:6] + (total[32:35] + total[44:47]))
        low = total[48:60] + total[60:72]
        plain = total[8:11] + total[11:14] + low[0:3]
        moments = total[14:23] + total[23:32] + low[3:12]
        a = (centres_ref[:, here] - MIDDLE) * (SCALE / 2)
        w = weights_ref[:, here] * (-10.0 / SCALE**4)
        for j in range(3):
            terms = w * (a[j : j + 1] * plain - moments[3 * j : 3 * j + 3])
            grad_c[j : j + 1, here] = jnp.sum(terms, axis=0, keepdims=True)


def body(node_coords, node_sens, centre_coords, centre_weights, pair_list, pair_count):
    device = lax.axis_index("tile")
    tiles, _, nodes = node_coords.shape
    slots = pair_list.shape[1]
    blocks = centre_coords.shape[1] // CENTRE_BLOCK
    code = pair_list[0] * 8 + pair_list[1] + 1
    code = jnp.where(jnp.arange(slots) < pair_count[0], code, 0).astype(F32)
    code = jnp.pad(code[None, None], ((0, 0), (0, tiles - 1), (0, nodes - slots)))
    packed = jnp.concatenate([node_coords.transpose(1, 0, 2), node_sens.transpose(1, 0, 2), code], 0)
    near = [swap(packed, "tile", by, phase) for by, phase in ((2, 0), (1, 1), (2, 1), (1, 0))]
    first = (device * blocks).astype(jnp.int32).reshape(1)

    vmem = pl.BlockSpec(memory_space=pltpu.VMEM)
    smem = pl.BlockSpec(memory_space=pltpu.SMEM)

    def scratch(count):
        return [
            pltpu.VMEM((count, nodes, 64), BF16),
            pltpu.VMEM((count, 32, nodes), BF16),
            pltpu.VMEM((count, 32, nodes), F8),
            pltpu.VMEM((count // 8, 8, 128), F32),
            pltpu.VMEM((count // 8, nodes // 128, 64 * 8, 128), F32),
            pltpu.VMEM((8, 128), jnp.int32),
            pltpu.SMEM((8, 128), jnp.int32),
            pltpu.SemaphoreType.DMA,
            pltpu.VMEM((nodes, 256), F32),
            pltpu.VMEM((nodes, 256), F32),
            pltpu.VMEM((2, nodes, 256), BF16),
            pltpu.VMEM((2, nodes, 256), BF16),
            pltpu.VMEM((2, nodes, 256), F8),
            pltpu.VMEM((2, nodes, 256), F8),
        ]

    params = pltpu.CompilerParams(vmem_limit_bytes=40 << 20)
    total_type = jax.ShapeDtypeStruct((blocks, 72, 128), F32)
    own, table = pl.pallas_call(
        own_kernel,
        out_shape=(total_type, jax.ShapeDtypeStruct((blocks, 32, 128), BF16)),
        in_specs=[vmem, vmem, smem],
        out_specs=(vmem, vmem),
        scratch_shapes=scratch(tiles),
        compiler_params=params,
        cost_estimate=pl.CostEstimate(flops=10**9, bytes_accessed=10**6, transcendentals=0),
        name="own_pairs",
    )(packed, centre_coords, first)
    grads = jax.ShapeDtypeStruct(centre_coords.shape, F32)
    return pl.pallas_call(
        near_kernel,
        out_shape=(grads, grads),
        in_specs=[vmem] * 6 + [smem] + [vmem] * 2,
        out_specs=(vmem, vmem),
        scratch_shapes=[pltpu.VMEM((blocks, 72, 128), F32)] + scratch(4 * tiles),
        compiler_params=params,
        name="near_pairs",
    )(*near, centre_coords, centre_weights, first, own, table)


def solution(mesh):
    return jax.shard_map(
        body,
        mesh=mesh,
        in_specs=(
            P(("case", "tile"), None, None),
            P(("case", "tile"), None, None),
            P(None, ("case", "tile")),
            P(None, ("case", "tile")),
            P(None, ("case", "tile")),
            P(("case", "tile")),
        ),
        out_specs=(P(None, ("case", "tile")), P(None, ("case", "tile"))),
        check_vma=False,
    )
```
